128 devices in a mesh: gx: 32 (over z, x, y_lo), gy: 4 (over y_hi, core).
Axes of the slice: x: 4, y: 4 (y_hi: 2, y_lo: 2; y = y_hi * 2 + y_lo), z: 4, core: 2. Of those that a mesh axis runs over, the one named last changes fastest.
Arguments:
- fields: float32 [4, 128, 32, 512], P(None, 'gx', 'gy'), may hold values from -6 to 6
- velocity: float32 [3, 128, 32, 512], P(None, 'gx', 'gy'), may hold values from -4 to 4
- diffusion: float32 [4], replicated, may hold values from 0.1 to 0.6
- panel_owner: int32 [131072, 1], P(('gx', 'gy')), may hold values from 0 to 127; in each aligned block of 1024 rows (0 to 1023, 1024 to 2047, ...) at most 32 rows name the same one
- panel_cell: int32 [131072], P(('gx', 'gy')), may hold values from 0 to 16383
- panel_bins: int32 [16, 131072], P(None, ('gx', 'gy')), may hold values from 0 to 127
- panel_position: float32 [3, 131072], P(None, ('gx', 'gy')), may hold values from -1 to 1, as said below
- panel_area: float32 [131072], P(('gx', 'gy')), may hold values from 0.3 to 3
- observer_position: float32 [3, 2048], replicated, may hold values from -2 to 2.25, as said below
Outputs:
- advanced: float32 [4, 128, 32, 512], P(None, 'gx', 'gy')
- signal: float32 [2048, 128], P(('gx', 'gy'))
The draws below stay inside these ranges and needn't reach their ends.
Inputs may be any that keep to these rules, and one draw needn't show every extreme that they name: `panel_owner`: among the panels of one device at most 32 name the same brick, a bound that some block reaches; every brick is named somewhere. `panel_cell`: A cell of the owning brick, numbered (x * 8 + y) * 512 + z in that brick's own coordinates. `panel_position`: every panel's third coordinate is 0 or less. `observer_position`: every observer's third coordinate is 0.25 or more.
All inputs are finite; a program needn't handle non-finite values.
Results may differ from the reference program's by a relative error of at most 0.0029.
Values sent between devices are 32-bit elements; how exact they have to be, the bound alone decides.
No kernel may reach another device: no remote copies, remote signals or barrier semaphores. Data moves between devices by JAX's collectives and lax.ppermute only.
A program may use at most 128 MiB of HBM per device.

```python
import math
import jax
import jax.numpy as jnp
import numpy as np
from jax import lax

BX = 4
BY = 8
BZ = 512
P_DEV = 1024
OBS = 2048
BINS = 128
OB = 128
NB = 16
NX = 128
NY = 32
PANELS = 131072
CAP = 32
N_GY = 4
DEVICES = 128


def draw_panel_position(key, part):
    across_key, height_key = jax.random.split(key)
    across = jax.random.uniform(across_key, (2, PANELS), jnp.float32, -1.0, 1.0)
    height = jax.random.uniform(height_key, (1, PANELS), jnp.float32, -1.0, 0.0)
    return jnp.concatenate([across, height], axis=0)


def draw_observer_position(key, part):
    across_key, height_key = jax.random.split(key)
    across = jax.random.uniform(across_key, (2, OBS), jnp.float32, -2.0, 2.0)
    height = jax.random.uniform(height_key, (1, OBS), jnp.float32, 0.25, 2.25)
    return jnp.concatenate([across, height], axis=0)


def plant(result, own_key, smallest, top_value):
    longest = result.shape.index(max(result.shape))
    spots = []
    for shift in (0, 1):
        where = [jax.random.randint(jax.random.fold_in(own_key, axis), (), 0, length) for axis, length in enumerate(result.shape)]
        where[longest] = (where[longest] + shift) % result.shape[longest]
        spots.append(tuple(where))
    return result.at[spots[0]].set(smallest).at[spots[1]].set(top_value)


def steps_of(stream_key, extent, cuts, least, high):
    gain = 1.0
    for dim, shards_of in cuts:
        steps = jax.random.uniform(jax.random.fold_in(jax.random.fold_in(stream_key, 6), dim), (shards_of,), jnp.float32, least / len(cuts), high / len(cuts))
        gain = gain * jnp.repeat(jnp.exp(steps), extent[dim] // shards_of).reshape((-1,) + (1,) * (len(extent) - 1 - dim))
    return gain


def routed_block(rng, own, number, rows, number_of, top, reach, lean):
    sequence = jax.random.permutation(rng, number_of)
    packed, common = shares(number_of, rows * top, reach, lean, True), shares(number_of, rows * top, reach, lean, False)
    places = jnp.arange(number_of)

    def named(lengths, turn):
        used = int((lengths > 0).sum())
        fixed = max(1, used // 4)
        shifted = fixed + (places - fixed + turn * (used - fixed)) % max(1, number_of - fixed)
        return jnp.zeros((number_of,), jnp.int32).at[sequence[jnp.where(places < fixed, places, shifted)]].set(jnp.asarray(lengths, jnp.int32))

    lengths = jnp.where(number % 4 == 0, named(packed, number // 4), named(common, number - number // 4 - 1))
    mixed = jax.random.permutation(jax.random.fold_in(own, 3), number_of)
    giver, receiver = mixed[0:number_of // 2 * 2:2], mixed[1:number_of // 2 * 2:2]
    slack = jnp.minimum(lengths[giver] - 1, reach - lengths[receiver]) // 2
    slack = jnp.where((giver == sequence[0]) | (receiver == sequence[0]) | (lengths[receiver] == 0), 0, jnp.maximum(slack, 0))
    shifted = jax.random.randint(jax.random.fold_in(own, 4), (number_of // 2,), 0, 1 << 20) % (slack + 1)
    lengths = lengths.at[giver].add(-shifted).at[receiver].add(shifted)
    items = jnp.searchsorted(jnp.cumsum(lengths), jnp.arange(rows * top), side="right").astype(jnp.int32)
    listing = items.reshape(top, rows).T
    listing = listing[jax.random.permutation(jax.random.fold_in(own, 1), rows)]
    turn = jax.random.randint(jax.random.fold_in(own, 2), (rows, 1), 0, top)
    return jnp.take_along_axis(listing, (jnp.arange(top)[None, :] + turn) % top, axis=1)


def shares(amount, total, bound, lean, full):
    portions = [(1 << 20) // math.isqrt(rank ** lean) + 1 for rank in range(1, amount + 1)]
    largest = bound if full else min(bound, max(-(-total // amount), total * portions[0] // sum(portions)))
    least = 1 if total - largest >= amount - 1 else 0
    holding, rest = [largest] + [least] * (amount - 1), total - largest - least * (amount - 1)
    while rest > 0:
        candidates = [i for i in range(1, amount) if holding[i] < largest] or [i for i in range(1, amount) if holding[i] < bound]
        mass, left = sum([portions[i] for i in candidates]), rest
        for i in candidates:
            addition = min(bound - holding[i], max(1, left * portions[i] // mass), rest)
            holding[i] = holding[i] + addition
            rest = rest - addition
    return np.array(holding)


def centred(own_key, dims, scale, reach, cuts=(), held_as=jnp.bfloat16):
    entries = scale * jax.random.normal(own_key, dims, jnp.float32)
    if cuts:
        entries = entries * steps_of(own_key, dims, cuts, -0.22, 0.18)
    return jnp.clip(entries, -reach, reach).astype(held_as)


def setup_inputs(seed: int = 0) -> dict:
    key_of = jax.random.split(jax.random.key(seed), 10)
    fields = centred(key_of[0], (4, NX, NY, BZ), 1.0, 6.0, ((1, 32), (2, 4)), jnp.float32)
    velocity = centred(key_of[1], (3, NX, NY, BZ), 1.0, 4.0, ((1, 32), (2, 4)), jnp.float32)
    diffusion = jnp.clip(jnp.exp(jax.random.uniform(key_of[2], (4,), jnp.float32, math.log(0.1), math.log(0.6))), 0.1, 0.6)
    panel_owner_keys = jax.random.split(jax.random.fold_in(key_of[3], 1), PANELS // P_DEV)
    panel_owner_turns = jax.random.permutation(jax.random.fold_in(key_of[3], 3), PANELS // P_DEV)
    panel_owner = jax.vmap(lambda own, number: routed_block(jax.random.fold_in(key_of[3], 2), own, number, P_DEV, DEVICES, 1, CAP, 2))(panel_owner_keys, panel_owner_turns).reshape((PANELS, 1))
    panel_cell = plant(jax.random.randint(key_of[4], (PANELS,), 0, BX * BY * BZ), jax.random.fold_in(key_of[4], 1), 0, (BX * BY * BZ) - 1).astype(jnp.int32)
    panel_bins = plant(jax.random.randint(key_of[5], (NB, PANELS), 0, BINS), jax.random.fold_in(key_of[5], 1), 0, BINS - 1).astype(jnp.int32)
    panel_position = draw_panel_position(jax.random.fold_in(key_of[9], 71), 0)
    panel_area = jnp.clip(jnp.exp(math.log(3.0) - 2.3025851 * jax.random.uniform(key_of[7], (PANELS,), jnp.float32) ** steps_of(key_of[7], (PANELS,), ((0, 128),), -0.2, 0.2)), 0.3, 3.0)
    observer_position = draw_observer_position(jax.random.fold_in(key_of[9], 71), 0)
    return {"fields": fields, "velocity": velocity, "diffusion": diffusion, "panel_owner": panel_owner, "panel_cell": panel_cell, "panel_bins": panel_bins, "panel_position": panel_position, "panel_area": panel_area, "observer_position": observer_position}


time_step = 0.15

def axis_terms(center, ahead_one, ahead_two, behind_one, behind_two):
    first = (8.0 * (ahead_one - behind_one) - (ahead_two - behind_two)) / 12.0
    second = (16.0 * (ahead_one + behind_one) - (ahead_two + behind_two) - 30.0 * center) / 12.0
    return (first, second)

def rates(padded, velocity, diffusion):
    center = padded[:, 2:-2, 2:-2, :]
    first_x, second_x = axis_terms(center, padded[:, 3:-1, 2:-2, :], padded[:, 4:, 2:-2, :], padded[:, 1:-3, 2:-2, :], padded[:, :-4, 2:-2, :])
    first_y, second_y = axis_terms(center, padded[:, 2:-2, 3:-1, :], padded[:, 2:-2, 4:, :], padded[:, 2:-2, 1:-3, :], padded[:, 2:-2, :-4, :])
    first_z, second_z = axis_terms(center, jnp.roll(center, -1, axis=3), jnp.roll(center, -2, axis=3), jnp.roll(center, 1, axis=3), jnp.roll(center, 2, axis=3))
    advect = velocity[0][None] * first_x + velocity[1][None] * first_y + velocity[2][None] * first_z
    return -advect + diffusion[:, None, None, None] * (second_x + second_y + second_z)

def wrap_pad(values):
    return jnp.pad(values, ((0, 0), (2, 2), (2, 2), (0, 0)), mode='wrap')

def emission(samples, position, area, bins_block, observers, scale):
    delta = observers[:, None, :] - position[:, :, None]
    inverse = lax.rsqrt(lax.optimization_barrier(jnp.sum(delta * delta, axis=0)))
    along = samples[1][:, None] * delta[0] + samples[2][:, None] * delta[1] + samples[3][:, None] * delta[2]
    emitted = scale * area[:, None] * (samples[0][:, None] + along * inverse) * inverse
    return emitted.astype(jnp.bfloat16)

def reference(fields, velocity, diffusion, panel_owner, panel_cell, panel_bins, panel_position, panel_area, observer_position):
    middle = fields + time_step * rates(wrap_pad(fields), velocity, diffusion)
    advanced = 0.5 * fields + 0.5 * (middle + time_step * rates(wrap_pad(middle), velocity, diffusion))
    owner = panel_owner[:, 0]
    brick_x = owner // N_GY
    brick_y = owner % N_GY
    local_x = panel_cell // (BY * BZ)
    local_y = panel_cell // BZ % BY
    local_z = panel_cell % BZ
    samples = fields[:, brick_x * BX + local_x, brick_y * BY + local_y, local_z]
    scale = (BINS / PANELS) ** 0.5
    sample_blocks = samples.reshape(4, DEVICES, P_DEV).transpose(1, 0, 2)
    position_blocks = panel_position.reshape(3, DEVICES, P_DEV).transpose(1, 0, 2)
    area_blocks = panel_area.reshape(DEVICES, P_DEV)
    bin_blocks = panel_bins.reshape(NB, DEVICES, P_DEV).transpose(1, 0, 2)
    levels = jnp.arange(BINS, dtype=jnp.int32)

    def accumulate(total, pieces):
        sample_block, position_block, area_block, bins_block = pieces
        emitted = emission(sample_block, position_block, area_block, bins_block, observer_position, scale)
        shaped = emitted.reshape(P_DEV, NB, OB).astype(jnp.float32)
        onehot = (bins_block[:, :, None] == levels[None, None, :]).astype(jnp.float32)
        return (total + jnp.einsum('pbo,bpt->bot', shaped, onehot), None)
    start = jnp.zeros((NB, OB, BINS), jnp.float32)
    total, unused = lax.scan(accumulate, start, (sample_blocks, position_blocks, area_blocks, bin_blocks))
    return (advanced, total.reshape(OBS, BINS))
```

```python
import functools

import jax
import jax.numpy as jnp
from jax import lax
from jax.experimental import pallas as pl
from jax.experimental.pallas import tpu as pltpu
from jax.sharding import Mesh
from jax.sharding import PartitionSpec as P

OBS = 2048
BINS = 128
OB = 128
CAP = 32
TIME_STEP = 0.15
VMEM_LIMIT = 48 * 1024 * 1024
F32 = jnp.float32
BF16 = jnp.bfloat16
NT = (((1,), (1,)), ((), ()))
NN = (((1,), (0,)), ((), ()))


def dot(a, b, dims):
    return lax.dot_general(a, b, dims, preferred_element_type=F32)


def route_kernel(owner_ref, cell_ref, bins_ref, position_ref, area_ref, request_ref, shared_ref):
    panels = owner_ref.shape[1]
    chunk = 256
    ahead = lax.broadcasted_iota(jnp.int32, (chunk, 2 * chunk), 0)
    behind = lax.broadcasted_iota(jnp.int32, (chunk, 2 * chunk), 1)
    before = jnp.where((ahead < behind) | (behind >= chunk), 1.0, 0.0).astype(BF16)
    device = lax.broadcasted_iota(jnp.int32, (128, chunk), 0)
    place = device % CAP
    running = jnp.zeros((128, chunk), F32)
    table = jnp.zeros((128, 256), F32)
    for k in range(panels // chunk):
        span = slice(k * chunk, (k + 1) * chunk)
        owner = owner_ref[:, span]
        cell = cell_ref[:, span]
        hit = jnp.where(device == owner, 1.0, 0.0)
        hot = hit.astype(BF16)
        counted = dot(hot, before, NN)
        rank = jnp.sum(hit * (counted[:, :chunk] + running), axis=0, keepdims=True)
        running = running + counted[:, chunk:]
        mine = place == rank.astype(jnp.int32)
        high = jnp.where(mine, (cell >> 7).astype(F32), 0.0)
        low = jnp.where(mine, (cell & 127).astype(F32), 0.0)
        table = table + dot(hot, jnp.concatenate([high, low], axis=0).astype(BF16), NT)
        for member in range(4):
            shared_ref[member, 8:9, span] = owner.astype(F32)
            shared_ref[member, 9:10, span] = rank
    request_ref[...] = (table[:, :128] * 128.0 + table[:, 128:]).astype(jnp.int32)
    for member in range(4):
        shared_ref[member, 0:4, :] = bins_ref[4 * member : 4 * member + 4, :].astype(F32)
        shared_ref[member, 4:7, :] = position_ref[...]
        shared_ref[member, 7:8, :] = area_ref[...]
        shared_ref[member, 10:16, :] = jnp.zeros((6, panels), F32)


def lookup(tile_of, lane, key):
    lanes = jnp.broadcast_to(lane, (8, 128))
    spot = jnp.broadcast_to(key, (8, 128)) - lax.broadcasted_iota(jnp.int32, (8, 128), 0)
    found = [jnp.zeros((8, 128), F32) for _ in range(4)]
    for tile in range(16):
        here = spot == tile * 8
        for c in range(4):
            taken = jnp.take_along_axis(tile_of(c, tile), lanes, axis=1)
            found[c] = jnp.where(here, taken, found[c])
    return [jnp.sum(f, axis=0, keepdims=True) for f in found]


def owner_kernel(arrived_ref, fields_ref, reply_ref):
    group = lax.broadcasted_iota(jnp.int32, (8, 128), 1) // CAP

    def tile_of(c, tile):
        return fields_ref[c, tile // 4, :, (tile % 4) * 128 : (tile % 4 + 1) * 128]

    def eight(k, carry):
        cells = jnp.zeros((8, 128), jnp.int32)
        for member in range(4):
            start = pl.multiple_of(k * 8 + member * 32, 8)
            cells = jnp.where(group == member, arrived_ref[pl.ds(start, 8), :], cells)
        found = []
        for row in range(8):
            cell = cells[row : row + 1]
            high = cell >> 7
            key = ((high >> 5) * 4 + (high & 3)) * 8 + ((high >> 2) & 7)
            found.append(lookup(tile_of, cell & 127, key))
        for c in range(4):
            block = jnp.concatenate([f[c] for f in found], axis=0)
            for member in range(4):
                start = pl.multiple_of(k * 8 + member * 32, 8)
                reply_ref[pl.ds(start, 8), c * 128 : (c + 1) * 128] = block
        return carry

    lax.fori_loop(0, 4, eight, 0)


def thirds(x):
    high = x.astype(BF16).astype(F32)
    rest = x - high
    middle = rest.astype(BF16).astype(F32)
    low = (rest - middle).astype(BF16).astype(F32)
    return high, middle, low


def emit_kernel(scale, returned_ref, shared_ref, observer_ref, signal_ref, along_ref, still_ref, square_ref):
    members, _, panels = shared_ref.shape
    zero = jnp.zeros((1, 128), F32)

    def tile_of(c, tile):
        return returned_ref[tile * 8 : tile * 8 + 8, c * 128 : (c + 1) * 128]

    def gather(k, carry):
        member = k // (panels // 128)
        inside = pl.multiple_of((k % (panels // 128)) * 128, 128)
        outside = pl.multiple_of(k * 128, 128)
        block = shared_ref[member, :, pl.ds(inside, 128)]
        owner = block[8:9].astype(jnp.int32)
        rank = block[9:10].astype(jnp.int32)
        s = lookup(tile_of, member * CAP + rank, owner)
        px, py, pz = block[4:5], block[5:6], block[6:7]
        area = block[7:8] * scale
        s = [area * v for v in s]
        along = jnp.concatenate(
            [s[1], s[2], s[3], -(s[1] * px + s[2] * py + s[3] * pz), zero, zero, zero, zero], axis=0
        )
        square = jnp.concatenate(
            [-2.0 * px, -2.0 * py, -2.0 * pz, px * px + py * py + pz * pz, zero + 1.0, zero, zero, zero],
            axis=0,
        )
        still_ref[:, pl.ds(outside, 128)] = s[0]
        for value, ref in ((along, along_ref), (square, square_ref)):
            h, m, w = thirds(value)
            ref[:, pl.ds(outside, 128)] = jnp.concatenate([h, h, m, m, h, w], axis=0).astype(BF16)
        return carry

    lax.fori_loop(0, members * panels // 128, gather, 0)

    ox, oy, oz = observer_ref[0:1, :], observer_ref[1:2, :], observer_ref[2:3, :]
    none = jnp.zeros_like(ox)
    features = jnp.concatenate(
        [ox, oy, oz, none + 1.0, ox * ox + oy * oy + oz * oz, none, none, none], axis=0
    )
    h, m, w = thirds(features)
    seen = jnp.transpose(jnp.concatenate([h, m, h, m, w, h], axis=0)).astype(BF16)

    chunk = 512
    level = lax.broadcasted_iota(jnp.int32, (BINS, chunk), 0).astype(F32)
    signal_ref[...] = jnp.zeros_like(signal_ref)

    def accumulate(k, carry):
        member = k // (panels // chunk)
        inside = pl.multiple_of((k % (panels // chunk)) * chunk, chunk)
        outside = pl.multiple_of(k * chunk, chunk)
        along_all = along_ref[:, pl.ds(outside, chunk)]
        square_all = square_ref[:, pl.ds(outside, chunk)]
        still = still_ref[:, pl.ds(outside, chunk)]
        bins = shared_ref[member, 0:4, pl.ds(inside, chunk)]
        for b in range(4):
            rows = slice(b * OB, (b + 1) * OB)
            inverse = lax.rsqrt(dot(seen[rows], square_all, NN))
            along = dot(seen[rows], along_all, NN)
            emitted = ((along * inverse + still) * inverse).astype(BF16)
            hot = jnp.where(bins[b : b + 1] == level, 1.0, 0.0).astype(BF16)
            signal_ref[rows, :] += dot(emitted, hot, NT)
        return carry

    lax.fori_loop(0, members * panels // chunk, accumulate, 0)


def rate_at(ref, x_low, x_high, y_low, y_high, velocity_ref, diffusion_ref, c, x):
    width = ref.shape[3]

    def column(i):
        if i < 0:
            return x_low[c, i + 2]
        if i >= 4:
            return x_high[c, i - 4]
        return ref[c, i]

    center = ref[c, x]
    tall = jnp.concatenate([y_low[c, x], center, y_high[c, x]], axis=0)
    near = [
        (column(x + 1), column(x - 1)),
        (tall[3:11], tall[1:9]),
        (pltpu.roll(center, width - 1, 1), pltpu.roll(center, 1, 1)),
    ]
    far = [
        (column(x + 2), column(x - 2)),
        (tall[4:12], tall[0:8]),
        (pltpu.roll(center, width - 2, 1), pltpu.roll(center, 2, 1)),
    ]
    advect = 0.0
    spread = -90.0 * center
    for k in range(3):
        advect = advect + velocity_ref[k, x] * (
            8.0 * (near[k][0] - near[k][1]) - (far[k][0] - far[k][1])
        )
        spread = spread + (16.0 * (near[k][0] + near[k][1]) - (far[k][0] + far[k][1]))
    return (diffusion_ref[c] * spread - advect) * (1.0 / 12.0)


def first_kernel(
    diffusion_ref, ref, xl, xh, yl, yh, velocity_ref, middle_ref, head_x, tail_x, head_y, tail_y
):
    for x in range(4):
        for c in range(4):
            value = ref[c, x] + TIME_STEP * rate_at(
                ref, xl, xh, yl, yh, velocity_ref, diffusion_ref, c, x
            )
            middle_ref[c, x] = value
            if x < 2:
                head_x[c, x] = value
            else:
                tail_x[c, x - 2] = value
            head_y[c, x] = value[0:2]
            tail_y[c, x] = value[6:8]


def second_kernel(diffusion_ref, fields_ref, ref, xl, xh, yl, yh, velocity_ref, out_ref):
    for x in range(4):
        for c in range(4):
            rate = rate_at(ref, xl, xh, yl, yh, velocity_ref, diffusion_ref, c, x)
            out_ref[c, x] = 0.5 * fields_ref[c, x] + 0.5 * (ref[c, x] + TIME_STEP * rate)


def neighbours(head_x, tail_x, head_y, tail_y):
    result = []
    for axis, count, head, tail in ((("hi", "lo"), 32, head_x, tail_x), ("gy", 4, head_y, tail_y)):
        result.append(lax.ppermute(tail, axis, [(i, (i + 1) % count) for i in range(count)]))
        result.append(lax.ppermute(head, axis, [((i + 1) % count, i) for i in range(count)]))
    return result


def exchange(array, axes):
    return lax.all_to_all(array, axes, split_axis=0, concat_axis=0, tiled=True)


VM = pl.BlockSpec(memory_space=pltpu.VMEM)
SM = pl.BlockSpec(memory_space=pltpu.SMEM)


def call(kernel, outs, in_specs, args, name, flops, moved, scratch=()):
    return pl.pallas_call(
        kernel,
        out_shape=outs,
        in_specs=in_specs,
        out_specs=jax.tree.map(lambda _: VM, outs),
        scratch_shapes=list(scratch),
        compiler_params=pltpu.CompilerParams(vmem_limit_bytes=VMEM_LIMIT),
        cost_estimate=pl.CostEstimate(flops=flops, bytes_accessed=moved, transcendentals=0),
        name=name,
    )(*args)


def per_device(
    fields,
    velocity,
    diffusion,
    panel_owner,
    panel_cell,
    panel_bins,
    panel_position,
    panel_area,
    observer_position,
):
    shape = jax.ShapeDtypeStruct
    panels = panel_cell.shape[0]
    both = ("hi", "lo", "gy")
    requests, shared = call(
        route_kernel,
        (shape((128, 128), jnp.int32), shape((4, 16, panels), F32)),
        [VM] * 5,
        (
            panel_owner.reshape(1, panels),
            panel_cell.reshape(1, panels),
            panel_bins,
            panel_position,
            panel_area.reshape(1, panels),
        ),
        "route",
        2_000_000,
        500_000,
    )
    arrived = exchange(requests, both)
    group = exchange(shared, "hi")
    observers = lax.dynamic_slice_in_dim(observer_position, lax.axis_index("hi") * 512, 512, 1)

    halos = neighbours(fields[:, :2], fields[:, 2:], fields[:, :, :2], fields[:, :, 6:])
    middle, *edges = call(
        first_kernel,
        (
            shape(fields.shape, F32),
            shape((4, 2, 8, 512), F32),
            shape((4, 2, 8, 512), F32),
            shape((4, 4, 2, 512), F32),
            shape((4, 4, 2, 512), F32),
        ),
        [SM] + [VM] * 6,
        (diffusion, fields, *halos, velocity),
        "first",
        4_000_000,
        2_000_000,
    )
    reply = call(
        owner_kernel,
        shape((128, 512), F32),
        [VM] * 2,
        (arrived, fields),
        "sample",
        4_000_000,
        600_000,
    )
    returned = exchange(reply, both)
    halos = neighbours(*edges)
    advanced = call(
        second_kernel,
        shape(fields.shape, F32),
        [SM] + [VM] * 7,
        (diffusion, fields, middle, *halos, velocity),
        "second",
        4_000_000,
        2_000_000,
    )
    scale = (BINS / (panels * 128)) ** 0.5
    partial = call(
        functools.partial(emit_kernel, scale),
        shape((512, BINS), F32),
        [VM] * 3,
        (returned, group, observers),
        "emit",
        600_000_000,
        800_000,
        (
            pltpu.VMEM((48, 4 * panels), BF16),
            pltpu.VMEM((1, 4 * panels), F32),
            pltpu.VMEM((48, 4 * panels), BF16),
        ),
    )
    return advanced, partial


def solution(mesh):
    count_x, count_y = mesh.devices.shape
    split = Mesh(mesh.devices.reshape(4, count_x // 4, count_y), ("hi", "lo", "gy"))
    gx = ("hi", "lo")
    every = ("hi", "lo", "gy")

    def whole(*args):
        advanced, partial = per_device(*args)
        parts = exchange(partial.reshape(32, 16, BINS), ("lo", "gy"))
        return advanced, jnp.sum(parts, axis=0)

    in_specs = (
        P(None, gx, "gy", None),
        P(None, gx, "gy", None),
        P(),
        P(every, None),
        P(every),
        P(None, every),
        P(None, every),
        P(every),
        P(),
    )
    out_specs = (P(None, gx, "gy", None), P(every, None))
    return jax.shard_map(whole, mesh=split, in_specs=in_specs, out_specs=out_specs, check_vma=False)
```

```python
import functools

import jax
import jax.numpy as jnp
from jax import lax
from jax.experimental import pallas as pl
from jax.experimental.pallas import tpu as pltpu
from jax.sharding import Mesh
from jax.sharding import PartitionSpec as P

OBS = 2048
BINS = 128
OB = 128
CAP = 32
TIME_STEP = 0.15
VMEM_LIMIT = 48 * 1024 * 1024
F32 = jnp.float32
BF16 = jnp.bfloat16
NT = (((1,), (1,)), ((), ()))
NN = (((1,), (0,)), ((), ()))


def dot(a, b, dims):
    return lax.dot_general(a, b, dims, preferred_element_type=F32)


def ask_kernel(owner_ref, cell_ref, request_ref, place_ref):
    panels = owner_ref.shape[1]
    chunk = 256
    ahead = lax.broadcasted_iota(jnp.int32, (chunk, 2 * chunk), 0)
    behind = lax.broadcasted_iota(jnp.int32, (chunk, 2 * chunk), 1)
    before = jnp.where((ahead < behind) | (behind >= chunk), 1.0, 0.0).astype(BF16)
    device = lax.broadcasted_iota(jnp.int32, (128, chunk), 0)
    place = device % CAP
    running = jnp.zeros((128, chunk), F32)
    table = jnp.zeros((128, 256), F32)
    for k in range(panels // chunk):
        span = slice(k * chunk, (k + 1) * chunk)
        owner = owner_ref[:, span]
        cell = cell_ref[:, span]
        hit = jnp.where(device == owner, 1.0, 0.0)
        hot = hit.astype(BF16)
        counted = dot(hot, before, NN)
        rank = jnp.sum(hit * (counted[:, :chunk] + running), axis=0, keepdims=True)
        running = running + counted[:, chunk:]
        mine = place == rank.astype(jnp.int32)
        high = jnp.where(mine, (cell >> 7).astype(F32), 0.0)
        low = jnp.where(mine, (cell & 127).astype(F32), 0.0)
        table = table + dot(hot, jnp.concatenate([high, low], axis=0).astype(BF16), NT)
        place_ref[0:1, span] = owner.astype(F32)
        place_ref[1:2, span] = rank
        place_ref[2:8, span] = jnp.zeros((6, chunk), F32)
    request_ref[...] = (table[:, :128] * 128.0 + table[:, 128:]).astype(jnp.int32)


def pack_kernel(place_ref, bins_ref, position_ref, area_ref, shared_ref):
    for member in range(4):
        shared_ref[member, 0:4, :] = bins_ref[4 * member : 4 * member + 4, :].astype(F32)
        shared_ref[member, 4:7, :] = position_ref[...]
        shared_ref[member, 7:8, :] = area_ref[...]
        shared_ref[member, 8:16, :] = place_ref[...]


def lookup(tile_of, lane, key):
    lanes = jnp.broadcast_to(lane, (8, 128))
    spot = jnp.broadcast_to(key, (8, 128)) - lax.broadcasted_iota(jnp.int32, (8, 128), 0)
    found = [jnp.zeros((8, 128), F32) for _ in range(4)]
    for tile in range(16):
        here = spot == tile * 8
        for c in range(4):
            taken = jnp.take_along_axis(tile_of(c, tile), lanes, axis=1)
            found[c] = jnp.where(here, taken, found[c])
    return [jnp.sum(f, axis=0, keepdims=True) for f in found]


def owner_kernel(arrived_ref, fields_ref, reply_ref):
    group = lax.broadcasted_iota(jnp.int32, (8, 128), 1) // CAP

    def tile_of(c, tile):
        return fields_ref[c, tile // 4, :, (tile % 4) * 128 : (tile % 4 + 1) * 128]

    def eight(k, carry):
        cells = jnp.zeros((8, 128), jnp.int32)
        for member in range(4):
            start = pl.multiple_of(k * 8 + member * 32, 8)
            cells = jnp.where(group == member, arrived_ref[pl.ds(start, 8), :], cells)
        found = []
        for row in range(8):
            cell = cells[row : row + 1]
            high = cell >> 7
            key = ((high >> 5) * 4 + (high & 3)) * 8 + ((high >> 2) & 7)
            found.append(lookup(tile_of, cell & 127, key))
        for c in range(4):
            block = jnp.concatenate([f[c] for f in found], axis=0)
            for member in range(4):
                start = pl.multiple_of(k * 8 + member * 32, 8)
                reply_ref[pl.ds(start, 8), c * 128 : (c + 1) * 128] = block
        return carry

    lax.fori_loop(0, 4, eight, 0)


def thirds(x):
    high = x.astype(BF16).astype(F32)
    rest = x - high
    middle = rest.astype(BF16).astype(F32)
    low = (rest - middle).astype(BF16).astype(F32)
    return high, middle, low


def emit_kernel(scale, returned_ref, shared_ref, observer_ref, signal_ref):
    members, _, panels = shared_ref.shape
    ox, oy, oz = observer_ref[0:1, :], observer_ref[1:2, :], observer_ref[2:3, :]
    none = jnp.zeros_like(ox)
    features = jnp.concatenate(
        [ox, oy, oz, none + 1.0, ox * ox + oy * oy + oz * oz, none, none, none], axis=0
    )
    h, m, w = thirds(features)
    seen = jnp.transpose(jnp.concatenate([h, m, h, m, w, h], axis=0)).astype(BF16)

    table = thirds(jnp.transpose(returned_ref[...]))
    device = lax.broadcasted_iota(jnp.int32, (128, panels), 0).astype(F32)
    place = lax.broadcasted_iota(jnp.int32, (CAP, panels), 0).astype(F32)
    level = lax.broadcasted_iota(jnp.int32, (BINS, panels), 0).astype(F32)
    zero = jnp.zeros((1, panels), F32)
    for member in range(members):
        mine = [
            jnp.concatenate(
                [part[c * 128 + member * CAP :][:CAP] for c in range(4)],
                axis=0,
            )
            for part in table
        ]
        rows = jnp.concatenate(mine, axis=1).astype(BF16)
        hot = jnp.where(device == shared_ref[member, 8:9, :], 1.0, 0.0).astype(BF16)
        looked = dot(rows, jnp.concatenate([hot, hot, hot], axis=0), NN)
        here = place == shared_ref[member, 9:10, :]
        area = shared_ref[member, 7:8, :] * scale
        s = [
            area
            * jnp.sum(jnp.where(here, looked[c * CAP : (c + 1) * CAP], 0.0), axis=0, keepdims=True)
            for c in range(4)
        ]
        px, py, pz = (shared_ref[member, k : k + 1, :] for k in (4, 5, 6))
        along = jnp.concatenate(
            [s[1], s[2], s[3], -(s[1] * px + s[2] * py + s[3] * pz), zero, zero, zero, zero], axis=0
        )
        square = jnp.concatenate(
            [-2.0 * px, -2.0 * py, -2.0 * pz, px * px + py * py + pz * pz, zero + 1.0, zero, zero, zero],
            axis=0,
        )
        h, m, w = thirds(along)
        along = dot(seen, jnp.concatenate([h, h, m, m, h, w], axis=0).astype(BF16), NN)
        h, m, w = thirds(square)
        square = dot(seen, jnp.concatenate([h, h, m, m, h, w], axis=0).astype(BF16), NN)
        inverse = lax.rsqrt(square)
        emitted = ((along * inverse + s[0]) * inverse).astype(BF16)
        for b in range(4):
            span = slice(b * OB, (b + 1) * OB)
            hot = jnp.where(shared_ref[member, b : b + 1, :] == level, 1.0, 0.0).astype(BF16)
            term = dot(emitted[span], hot, NT)
            signal_ref[span, :] = term if member == 0 else signal_ref[span, :] + term


def rate_at(ref, x_low, x_high, y_low, y_high, velocity_ref, diffusion_ref, c, x):
    width = ref.shape[3]

    def column(i):
        if i < 0:
            return x_low[c, i + 2]
        if i >= 4:
            return x_high[c, i - 4]
        return ref[c, i]

    center = ref[c, x]
    tall = jnp.concatenate([y_low[c, x], center, y_high[c, x]], axis=0)
    near = [
        (column(x + 1), column(x - 1)),
        (tall[3:11], tall[1:9]),
        (pltpu.roll(center, width - 1, 1), pltpu.roll(center, 1, 1)),
    ]
    far = [
        (column(x + 2), column(x - 2)),
        (tall[4:12], tall[0:8]),
        (pltpu.roll(center, width - 2, 1), pltpu.roll(center, 2, 1)),
    ]
    advect = 0.0
    spread = -90.0 * center
    for k in range(3):
        advect = advect + velocity_ref[k, x] * (
            8.0 * (near[k][0] - near[k][1]) - (far[k][0] - far[k][1])
        )
        spread = spread + (16.0 * (near[k][0] + near[k][1]) - (far[k][0] + far[k][1]))
    return (diffusion_ref[c] * spread - advect) * (1.0 / 12.0)


def first_kernel(
    diffusion_ref, ref, xl, xh, yl, yh, velocity_ref, middle_ref, head_x, tail_x, head_y, tail_y
):
    for x in range(4):
        for c in range(4):
            value = ref[c, x] + TIME_STEP * rate_at(
                ref, xl, xh, yl, yh, velocity_ref, diffusion_ref, c, x
            )
            middle_ref[c, x] = value
            if x < 2:
                head_x[c, x] = value
            else:
                tail_x[c, x - 2] = value
            head_y[c, x] = value[0:2]
            tail_y[c, x] = value[6:8]


def second_kernel(diffusion_ref, fields_ref, ref, xl, xh, yl, yh, velocity_ref, out_ref):
    for x in range(4):
        for c in range(4):
            rate = rate_at(ref, xl, xh, yl, yh, velocity_ref, diffusion_ref, c, x)
            out_ref[c, x] = 0.5 * fields_ref[c, x] + 0.5 * (ref[c, x] + TIME_STEP * rate)


def neighbours(head_x, tail_x, head_y, tail_y):
    result = []
    for axis, count, head, tail in ((("hi", "lo"), 32, head_x, tail_x), ("gy", 4, head_y, tail_y)):
        result.append(lax.ppermute(tail, axis, [(i, (i + 1) % count) for i in range(count)]))
        result.append(lax.ppermute(head, axis, [((i + 1) % count, i) for i in range(count)]))
    return result


def exchange(array, axes):
    return lax.all_to_all(array, axes, split_axis=0, concat_axis=0, tiled=True)


VM = pl.BlockSpec(memory_space=pltpu.VMEM)
SM = pl.BlockSpec(memory_space=pltpu.SMEM)


def call(kernel, outs, in_specs, args, name, flops, moved, limit=VMEM_LIMIT):
    return pl.pallas_call(
        kernel,
        out_shape=outs,
        in_specs=in_specs,
        out_specs=jax.tree.map(lambda _: VM, outs),
        compiler_params=pltpu.CompilerParams(vmem_limit_bytes=limit),
        cost_estimate=pl.CostEstimate(flops=flops, bytes_accessed=moved, transcendentals=0),
        name=name,
    )(*args)


def ask(owner, cell):
    panels = owner.shape[1]
    row = pl.BlockSpec((1, panels), lambda i: (0, 0))
    return pl.pallas_call(
        ask_kernel,
        grid=(1,),
        out_shape=(
            jax.ShapeDtypeStruct((128, 128), jnp.int32),
            jax.ShapeDtypeStruct((8, panels), F32),
        ),
        in_specs=[row, row],
        out_specs=(
            pl.BlockSpec((128, 128), lambda i: (0, 0)),
            pl.BlockSpec((8, panels), lambda i: (0, 0)),
        ),
        cost_estimate=pl.CostEstimate(flops=2_000_000, bytes_accessed=100_000, transcendentals=0),
        compiler_params=pltpu.CompilerParams(vmem_limit_bytes=16 * 1024 * 1024),
        name="ask",
    )(owner, cell)


def per_device(
    fields,
    velocity,
    diffusion,
    panel_owner,
    panel_cell,
    panel_bins,
    panel_position,
    panel_area,
    observer_position,
):
    shape = jax.ShapeDtypeStruct
    after = lax.optimization_barrier
    panels = panel_cell.shape[0]
    every = ("hi", "lo", "gy")
    strips = (
        shape((4, 2, 8, 512), F32),
        shape((4, 2, 8, 512), F32),
        shape((4, 4, 2, 512), F32),
        shape((4, 4, 2, 512), F32),
    )

    requests, place = ask(panel_owner.reshape(1, panels), panel_cell.reshape(1, panels))
    arrived = exchange(requests, every)

    place, cells, _ = after((place, fields, requests))
    shared = call(
        pack_kernel,
        shape((4, 16, panels), F32),
        [VM] * 4,
        (place, panel_bins, panel_position, panel_area.reshape(1, panels)),
        "pack",
        100_000,
        500_000,
    )
    group = exchange(shared, "hi")
    observers = lax.dynamic_slice_in_dim(observer_position, lax.axis_index("hi") * 512, 512, 1)
    halos = neighbours(cells[:, :2], cells[:, 2:], cells[:, :, :2], cells[:, :, 6:])
    arrived, group, observers, *halos = after((arrived, group, observers, *halos))

    reply = call(
        owner_kernel,
        shape((128, 512), F32),
        [VM] * 2,
        (arrived, fields),
        "sample",
        4_000_000,
        600_000,
    )
    returned = exchange(reply, every)

    halos = after((reply, *halos))[1:]
    middle, *edges = call(
        first_kernel,
        (shape(fields.shape, F32), *strips),
        [SM] + [VM] * 6,
        (diffusion, fields, *halos, velocity),
        "first",
        4_000_000,
        2_000_000,
    )
    halos = neighbours(*edges)
    returned, *halos = after((returned, *halos))

    scale = (BINS / (panels * 128)) ** 0.5
    partial = call(
        functools.partial(emit_kernel, scale),
        shape((512, BINS), F32),
        [VM] * 3,
        (returned, group, observers),
        "emit",
        600_000_000,
        800_000,
    )
    parts = exchange(partial.reshape(32, 16, BINS), ("lo", "gy"))

    halos = after((partial, *halos))[1:]
    advanced = call(
        second_kernel,
        shape(fields.shape, F32),
        [SM] + [VM] * 7,
        (diffusion, fields, middle, *halos, velocity),
        "second",
        4_000_000,
        2_000_000,
    )
    parts, advanced = after((parts, advanced))
    return advanced, jnp.sum(parts, axis=0)


def solution(mesh):
    count_x, count_y = mesh.devices.shape
    split = Mesh(mesh.devices.reshape(4, count_x // 4, count_y), ("hi", "lo", "gy"))
    gx = ("hi", "lo")
    every = ("hi", "lo", "gy")

    in_specs = (
        P(None, gx, "gy", None),
        P(None, gx, "gy", None),
        P(),
        P(every, None),
        P(every),
        P(None, every),
        P(None, every),
        P(every),
        P(),
    )
    out_specs = (P(None, gx, "gy", None), P(every, None))
    return jax.shard_map(
        per_device, mesh=split, in_specs=in_specs, out_specs=out_specs, check_vma=False
    )
```

```python
import functools

import jax
import jax.numpy as jnp
from jax import lax
from jax.experimental import pallas as pl
from jax.experimental.pallas import tpu as pltpu
from jax.sharding import Mesh
from jax.sharding import PartitionSpec as P

OBS = 2048
BINS = 128
OB = 128
CAP = 32
TIME_STEP = 0.15
VMEM_LIMIT = 48 * 1024 * 1024
F32 = jnp.float32
BF16 = jnp.bfloat16
NT = (((1,), (1,)), ((), ()))
NN = (((1,), (0,)), ((), ()))


def dot(a, b, dims):
    return lax.dot_general(a, b, dims, preferred_element_type=F32)


def ask_kernel(owner_ref, cell_ref, request_ref, place_ref):
    panels = owner_ref.shape[1]
    chunk = 256
    ahead = lax.broadcasted_iota(jnp.int32, (chunk, 2 * chunk), 0)
    behind = lax.broadcasted_iota(jnp.int32, (chunk, 2 * chunk), 1)
    before = jnp.where((ahead < behind) | (behind >= chunk), 1.0, 0.0).astype(BF16)
    device = lax.broadcasted_iota(jnp.int32, (128, chunk), 0)
    place = device % CAP
    running = jnp.zeros((128, chunk), F32)
    table = jnp.zeros((128, 256), F32)
    for k in range(panels // chunk):
        span = slice(k * chunk, (k + 1) * chunk)
        owner = owner_ref[:, span]
        cell = cell_ref[:, span]
        hit = jnp.where(device == owner, 1.0, 0.0)
        hot = hit.astype(BF16)
        counted = dot(hot, before, NN)
        rank = jnp.sum(hit * (counted[:, :chunk] + running), axis=0, keepdims=True)
        running = running + counted[:, chunk:]
        mine = place == rank.astype(jnp.int32)
        high = jnp.where(mine, (cell >> 7).astype(F32), 0.0)
        low = jnp.where(mine, (cell & 127).astype(F32), 0.0)
        table = table + dot(hot, jnp.concatenate([high, low], axis=0).astype(BF16), NT)
        place_ref[0:1, span] = owner.astype(F32)
        place_ref[1:2, span] = rank
        place_ref[2:8, span] = jnp.zeros((6, chunk), F32)
    request_ref[...] = (table[:, :128] * 128.0 + table[:, 128:]).astype(jnp.int32)


def pack_kernel(
    at_ref, place_ref, bins_ref, position_ref, area_ref, fields_ref, velocity_ref, *outs
):
    for k in range(4):
        to = (at_ref[0] + (4 - k)) % 4
        rows = jnp.zeros((4, bins_ref.shape[1]), F32)
        for member in range(4):
            rows = jnp.where(
                to == member, bins_ref[4 * member : 4 * member + 4, :].astype(F32), rows
            )
        outs[k][0:4, :] = rows
        outs[k][4:7, :] = position_ref[...]
        outs[k][7:8, :] = area_ref[...]
        outs[k][8:16, :] = place_ref[...]
    head, tail = outs[4], outs[5]
    for c in range(4):
        for x in range(4):
            head[4 * c + x] = fields_ref[c, x]
            tail[4 * c + x] = fields_ref[c, x]
    for k in range(3):
        for x in range(2):
            head[16 + 2 * k + x] = velocity_ref[k, x]
            tail[16 + 2 * k + x] = velocity_ref[k, x + 2]


def lookup(tile_of, lane, key):
    lanes = jnp.broadcast_to(lane, (8, 128))
    spot = jnp.broadcast_to(key, (8, 128)) - lax.broadcasted_iota(jnp.int32, (8, 128), 0)
    found = [jnp.zeros((8, 128), F32) for _ in range(4)]
    for tile in range(16):
        here = spot == tile * 8
        for c in range(4):
            taken = jnp.take_along_axis(tile_of(c, tile), lanes, axis=1)
            found[c] = jnp.where(here, taken, found[c])
    return [jnp.sum(f, axis=0, keepdims=True) for f in found]


def owner_kernel(arrived_ref, fields_ref, reply_ref):
    group = lax.broadcasted_iota(jnp.int32, (8, 128), 1) // CAP

    def tile_of(c, tile):
        return fields_ref[c, tile // 4, :, (tile % 4) * 128 : (tile % 4 + 1) * 128]

    def eight(k, carry):
        cells = jnp.zeros((8, 128), jnp.int32)
        for member in range(4):
            start = pl.multiple_of(k * 8 + member * 32, 8)
            cells = jnp.where(group == member, arrived_ref[pl.ds(start, 8), :], cells)
        found = []
        for row in range(8):
            cell = cells[row : row + 1]
            high = cell >> 7
            key = ((high >> 5) * 4 + (high & 3)) * 8 + ((high >> 2) & 7)
            found.append(lookup(tile_of, cell & 127, key))
        for row in range(8):
            block = jnp.concatenate(found[row], axis=0)
            for member in range(4):
                turned = block if member == 0 else pltpu.roll(block, 128 - CAP * member, 1)
                reply_ref[k * 8 + (member * 32 + row)] = turned
        return carry

    lax.fori_loop(0, 4, eight, 0)


def thirds(x):
    high = x.astype(BF16).astype(F32)
    rest = x - high
    middle = rest.astype(BF16).astype(F32)
    low = (rest - middle).astype(BF16).astype(F32)
    return high, middle, low


def emit_kernel(scale, returned_ref, *refs):
    *shared_refs, observer_ref, signal_ref = refs
    members = len(shared_refs)
    panels = shared_refs[0].shape[1]
    ox, oy, oz = observer_ref[0:1, :], observer_ref[1:2, :], observer_ref[2:3, :]
    none = jnp.zeros_like(ox)
    features = jnp.concatenate(
        [ox, oy, oz, none + 1.0, ox * ox + oy * oy + oz * oz, none, none, none], axis=0
    )
    h, m, w = thirds(features)
    seen = jnp.transpose(jnp.concatenate([h, m, h, m, w, h], axis=0)).astype(BF16)

    table = thirds(
        jnp.concatenate([jnp.transpose(returned_ref[:, c, :]) for c in range(4)], axis=0)
    )
    device = lax.broadcasted_iota(jnp.int32, (128, panels), 0).astype(F32)
    place = lax.broadcasted_iota(jnp.int32, (CAP, panels), 0).astype(F32)
    level = lax.broadcasted_iota(jnp.int32, (BINS, panels), 0).astype(F32)
    zero = jnp.zeros((1, panels), F32)
    for member in range(members):
        shared_ref = shared_refs[member]
        mine = [
            jnp.concatenate(
                [part[c * 128 + member * CAP :][:CAP] for c in range(4)],
                axis=0,
            )
            for part in table
        ]
        rows = jnp.concatenate(mine, axis=1).astype(BF16)
        hot = jnp.where(device == shared_ref[8:9, :], 1.0, 0.0).astype(BF16)
        looked = dot(rows, jnp.concatenate([hot, hot, hot], axis=0), NN)
        here = place == shared_ref[9:10, :]
        area = shared_ref[7:8, :] * scale
        s = [
            area
            * jnp.sum(jnp.where(here, looked[c * CAP : (c + 1) * CAP], 0.0), axis=0, keepdims=True)
            for c in range(4)
        ]
        px, py, pz = (shared_ref[k : k + 1, :] for k in (4, 5, 6))
        along = jnp.concatenate(
            [s[1], s[2], s[3], -(s[1] * px + s[2] * py + s[3] * pz), zero, zero, zero, zero], axis=0
        )
        square = jnp.concatenate(
            [-2.0 * px, -2.0 * py, -2.0 * pz, px * px + py * py + pz * pz, zero + 1.0, zero, zero, zero],
            axis=0,
        )
        h, m, w = thirds(along)
        along = dot(seen, jnp.concatenate([h, h, m, m, h, w], axis=0).astype(BF16), NN)
        h, m, w = thirds(square)
        square = dot(seen, jnp.concatenate([h, h, m, m, h, w], axis=0).astype(BF16), NN)
        inverse = lax.rsqrt(square)
        emitted = ((along * inverse + s[0]) * inverse).astype(BF16)
        for b in range(4):
            span = slice(b * OB, (b + 1) * OB)
            hot = jnp.where(shared_ref[b : b + 1, :] == level, 1.0, 0.0).astype(BF16)
            term = dot(emitted[span], hot, NT)
            signal_ref[span, :] = term if member == 0 else signal_ref[span, :] + term


def rim_kernel(fields_ref, velocity_ref, left_ref, right_ref, head_ref, tail_ref):
    for c in range(4):
        for x in range(-2, 6):
            column = column_of(fields_ref, left_ref, right_ref, c, x)
            head_ref[8 * c + x + 2] = column[0:4]
            tail_ref[8 * c + x + 2] = column[4:8]
    for k in range(3):
        for half in range(2):
            one, two = velocity_ref[k, 2 * half], velocity_ref[k, 2 * half + 1]
            head_ref[32 + 2 * k + half] = jnp.concatenate([one[0:2], two[0:2]], axis=0)
            tail_ref[32 + 2 * k + half] = jnp.concatenate([one[6:8], two[6:8]], axis=0)


def column_of(fields_ref, left_ref, right_ref, c, x):
    if x < 0:
        return left_ref[4 * c + x + 4]
    if x >= 4:
        return right_ref[4 * c + x - 4]
    return fields_ref[c, x]


def rate(center, across, tall, velocity, diffusion):
    rows, width = center.shape
    near = [
        (across[2], across[1]),
        (tall[3 : 3 + rows], tall[1 : 1 + rows]),
        (pltpu.roll(center, width - 1, 1), pltpu.roll(center, 1, 1)),
    ]
    far = [
        (across[3], across[0]),
        (tall[4 : 4 + rows], tall[0:rows]),
        (pltpu.roll(center, width - 2, 1), pltpu.roll(center, 2, 1)),
    ]
    advect = 0.0
    spread = -90.0 * center
    for k in range(3):
        advect = advect + velocity[k] * (
            8.0 * (near[k][0] - near[k][1]) - (far[k][0] - far[k][1])
        )
        spread = spread + (16.0 * (near[k][0] + near[k][1]) - (far[k][0] + far[k][1]))
    return (diffusion * spread - advect) * (1.0 / 12.0)


def transport_kernel(
    diffusion_ref, fields_ref, velocity_ref, left_ref, right_ref, low_ref, high_ref, out_ref
):
    for c in range(4):
        diffusion = diffusion_ref[c]

        def column(x):
            return column_of(fields_ref, left_ref, right_ref, c, x)

        tall = {
            x: jnp.concatenate(
                [low_ref[8 * c + x + 2][2:4], column(x), high_ref[8 * c + x + 2][0:2]], axis=0
            )
            for x in range(-2, 6)
        }
        middle = {}
        taller = {}
        for x in range(4):
            center = tall[x]
            wide = jnp.concatenate(
                [low_ref[8 * c + x + 2][0:2], center, high_ref[8 * c + x + 2][2:4]], axis=0
            )
            velocity = []
            for k in range(3):
                spot, part = 32 + 2 * k + x // 2, slice(2 * (x % 2), 2 * (x % 2) + 2)
                velocity.append(
                    jnp.concatenate(
                        [low_ref[spot][part], velocity_ref[k, x], high_ref[spot][part]], axis=0
                    )
                )
            across = [tall[x + d] for d in (-2, -1, 1, 2)]
            taller[x] = center + TIME_STEP * rate(center, across, wide, velocity, diffusion)
            middle[x] = taller[x][2:10]
        for x in (-2, -1, 4, 5):
            center = column(x)
            side, spot = (left_ref, x + 2) if x < 0 else (right_ref, x - 4)
            velocity = [side[16 + 2 * k + spot] for k in range(3)]
            across = [column(x + d) for d in (-2, -1, 1, 2)]
            middle[x] = center + TIME_STEP * rate(center, across, tall[x], velocity, diffusion)
        for x in range(4):
            velocity = [velocity_ref[k, x] for k in range(3)]
            across = [middle[x + d] for d in (-2, -1, 1, 2)]
            change = rate(middle[x], across, taller[x], velocity, diffusion)
            out_ref[c, x] = 0.5 * fields_ref[c, x] + 0.5 * (middle[x] + TIME_STEP * change)


def neighbours(axis, count, head, tail):
    return (
        lax.ppermute(tail, axis, [(i, (i + 1) % count) for i in range(count)]),
        lax.ppermute(head, axis, [((i + 1) % count, i) for i in range(count)]),
    )


def exchange(array, axes):
    return lax.all_to_all(array, axes, split_axis=0, concat_axis=0, tiled=True)


VM = pl.BlockSpec(memory_space=pltpu.VMEM)
SM = pl.BlockSpec(memory_space=pltpu.SMEM)


def call(kernel, outs, in_specs, args, name, flops, moved, limit=VMEM_LIMIT):
    return pl.pallas_call(
        kernel,
        out_shape=outs,
        in_specs=in_specs,
        out_specs=jax.tree.map(lambda _: VM, outs),
        compiler_params=pltpu.CompilerParams(vmem_limit_bytes=limit),
        cost_estimate=pl.CostEstimate(flops=flops, bytes_accessed=moved, transcendentals=0),
        name=name,
    )(*args)


def ask(owner, cell):
    panels = owner.shape[1]
    row = pl.BlockSpec((1, panels), lambda i: (0, 0))
    return pl.pallas_call(
        ask_kernel,
        grid=(1,),
        out_shape=(
            jax.ShapeDtypeStruct((128, 128), jnp.int32),
            jax.ShapeDtypeStruct((8, panels), F32),
        ),
        in_specs=[row, row],
        out_specs=(
            pl.BlockSpec((128, 128), lambda i: (0, 0)),
            pl.BlockSpec((8, panels), lambda i: (0, 0)),
        ),
        cost_estimate=pl.CostEstimate(flops=2_000_000, bytes_accessed=100_000, transcendentals=0),
        compiler_params=pltpu.CompilerParams(vmem_limit_bytes=16 * 1024 * 1024),
        name="ask",
    )(owner, cell)


def per_device(
    fields,
    velocity,
    diffusion,
    panel_owner,
    panel_cell,
    panel_bins,
    panel_position,
    panel_area,
    observer_position,
):
    shape = jax.ShapeDtypeStruct
    after = lax.optimization_barrier
    panels = panel_cell.shape[0]
    every = ("hi", "lo", "gy")
    share = shape((16, panels), F32)
    sides = shape((22, 8, 512), F32)
    rims = shape((38, 4, 512), F32)

    requests, place = ask(panel_owner.reshape(1, panels), panel_cell.reshape(1, panels))
    arrived = exchange(requests, every)

    at = lax.axis_index("hi")
    observers = lax.dynamic_slice_in_dim(observer_position, at * 512, 512, 1)
    place, _ = after((place, requests))
    *group, head, tail = call(
        pack_kernel,
        (share, share, share, share, sides, sides),
        [SM] + [VM] * 6,
        (
            at.reshape(1),
            place,
            panel_bins,
            panel_position,
            panel_area.reshape(1, panels),
            fields,
            velocity,
        ),
        "pack",
        100_000,
        2_000_000,
    )
    arrived = after((arrived, head, tail, *group))[0]
    left, right = neighbours(("hi", "lo"), 32, head, tail)
    for k in range(1, 4):
        group[k] = lax.ppermute(group[k], "hi", [(i, (i - k) % 4) for i in range(4)])

    reply = call(
        owner_kernel,
        shape((128, 4, 128), F32),
        [VM] * 2,
        (arrived, fields),
        "sample",
        5_000_000_000,
        600_000,
    )
    returned = exchange(reply, every)

    left, right, _ = after((left, right, reply))
    head, tail = call(
        rim_kernel,
        (rims, rims),
        [VM] * 4,
        (fields, velocity, left, right),
        "rim",
        100_000,
        2_000_000,
    )
    low, high = neighbours("gy", 4, head, tail)

    scale = (BINS / (panels * 128)) ** 0.5
    partial = call(
        functools.partial(emit_kernel, scale),
        shape((512, BINS), F32),
        [VM] * 6,
        (returned, *group, observers),
        "emit",
        600_000_000,
        800_000,
    )
    parts = exchange(partial.reshape(32, 16, BINS), ("lo", "gy"))

    low, high, _ = after((low, high, partial))
    advanced = call(
        transport_kernel,
        shape(fields.shape, F32),
        [SM] + [VM] * 6,
        (diffusion, fields, velocity, left, right, low, high),
        "transport",
        16_000_000,
        3_000_000,
    )
    parts, advanced = after((parts, advanced))
    return advanced, jnp.sum(parts, axis=0)


def solution(mesh):
    count_x, count_y = mesh.devices.shape
    split = Mesh(mesh.devices.reshape(4, count_x // 4, count_y), ("hi", "lo", "gy"))
    gx = ("hi", "lo")
    every = ("hi", "lo", "gy")

    in_specs = (
        P(None, gx, "gy", None),
        P(None, gx, "gy", None),
        P(),
        P(every, None),
        P(every),
        P(None, every),
        P(None, every),
        P(every),
        P(),
    )
    out_specs = (P(None, gx, "gy", None), P(every, None))
    return jax.shard_map(
        per_device, mesh=split, in_specs=in_specs, out_specs=out_specs, check_vma=False
    )
```

```python
import functools

import jax
import jax.numpy as jnp
from jax import lax
from jax.experimental import pallas as pl
from jax.experimental.pallas import tpu as pltpu
from jax.sharding import Mesh
from jax.sharding import PartitionSpec as P

OBS = 2048
BINS = 128
OB = 128
CAP = 32
TIME_STEP = 0.15
VMEM_LIMIT = 48 * 1024 * 1024
FULL_VMEM = 60 * 1024 * 1024
F32 = jnp.float32
BF16 = jnp.bfloat16
NT = (((1,), (1,)), ((), ()))
NN = (((1,), (0,)), ((), ()))


def dot(a, b, dims):
    return lax.dot_general(a, b, dims, preferred_element_type=F32)


def ask_kernel(owner_in, cell_in, request_ref, place_ref, owner_ref, cell_ref, arrival):
    loads = [
        pltpu.make_async_copy(owner_in, owner_ref, arrival.at[0]),
        pltpu.make_async_copy(cell_in, cell_ref, arrival.at[1]),
    ]
    for load in loads:
        load.start()
    panels = owner_ref.shape[1]
    chunk = 256
    ahead = lax.broadcasted_iota(jnp.int32, (chunk, 2 * chunk), 0)
    behind = lax.broadcasted_iota(jnp.int32, (chunk, 2 * chunk), 1)
    before = jnp.where((ahead < behind) | (behind >= chunk), 1.0, 0.0).astype(BF16)
    device = lax.broadcasted_iota(jnp.int32, (128, chunk), 0)
    place = device % CAP
    running = jnp.zeros((128, chunk), F32)
    table = jnp.zeros((128, 256), F32)
    for load in loads:
        load.wait()
    for k in range(panels // chunk):
        span = slice(k * chunk, (k + 1) * chunk)
        owner = owner_ref[:, span]
        cell = cell_ref[:, span]
        hit = jnp.where(device == owner, 1.0, 0.0)
        hot = hit.astype(BF16)
        counted = dot(hot, before, NN)
        rank = jnp.sum(hit * (counted[:, :chunk] + running), axis=0, keepdims=True)
        running = running + counted[:, chunk:]
        mine = place == rank.astype(jnp.int32)
        high = jnp.where(mine, (cell >> 7).astype(F32), 0.0)
        low = jnp.where(mine, (cell & 127).astype(F32), 0.0)
        table = table + dot(hot, jnp.concatenate([high, low], axis=0).astype(BF16), NT)
        place_ref[0:1, span] = owner.astype(F32)
        place_ref[1:2, span] = rank
        place_ref[2:8, span] = jnp.zeros((6, chunk), F32)
    request_ref[...] = (table[:, :128] * 128.0 + table[:, 128:]).astype(jnp.int32)


def pack_kernel(at_ref, place_ref, bins_ref, position_ref, area_ref, *outs):
    for k in range(4):
        to = (at_ref[0] + (4 - k)) % 4
        rows = jnp.zeros((4, bins_ref.shape[1]), F32)
        for member in range(4):
            rows = jnp.where(
                to == member, bins_ref[4 * member : 4 * member + 4, :].astype(F32), rows
            )
        outs[k][0:4, :] = rows
        outs[k][4:7, :] = position_ref[...]
        outs[k][7:8, :] = area_ref[...]
        outs[k][8:16, :] = place_ref[...]


def owner_kernel(arrived_ref, fields_ref, reply_ref):
    group = lax.broadcasted_iota(jnp.int32, (32, 128), 1) // CAP
    cells = jnp.zeros((32, 128), jnp.int32)
    for member in range(4):
        cells = jnp.where(group == member, arrived_ref[member * 32 : member * 32 + 32, :], cells)
    block = cells >> 7
    key = ((cells >> 6) & 1) * 128 + ((block >> 5) * 4 + (block & 3)) * 8 + ((block >> 2) & 7)
    spot = cells & 63

    tables = []
    for c in range(4):
        rows = jnp.concatenate(
            [fields_ref[c, x, :, z * 128 : (z + 1) * 128] for x in range(4) for z in range(4)],
            axis=0,
        )
        rows = jnp.transpose(rows)
        rows = jnp.concatenate([rows[:64], rows[64:]], axis=1)
        tables.append(jnp.concatenate(thirds(rows), axis=1).astype(BF16))
    table = jnp.concatenate(tables, axis=0)

    row = lax.broadcasted_iota(jnp.int32, (256, 128), 0)
    lane = lax.broadcasted_iota(jnp.int32, (64, 128), 0)
    for g in range(0, 32, 8):
        hot = jnp.concatenate(
            [jnp.where(row == key[g + j : g + j + 1], 1.0, 0.0).astype(BF16) for j in range(8)],
            axis=1,
        )
        looked = dot(table, jnp.concatenate([hot, hot, hot], axis=0), NN)
        for j in range(8):
            mine = lane == spot[g + j : g + j + 1]
            found = jnp.concatenate(
                [
                    jnp.sum(
                        jnp.where(mine, looked[c * 64 : c * 64 + 64, j * 128 : j * 128 + 128], 0.0),
                        axis=0,
                        keepdims=True,
                    )
                    for c in range(4)
                ],
                axis=0,
            )
            for member in range(4):
                turned = found if member == 0 else pltpu.roll(found, 128 - CAP * member, 1)
                reply_ref[member * 32 + g + j] = turned


def thirds(x):
    high = x.astype(BF16).astype(F32)
    rest = x - high
    middle = rest.astype(BF16).astype(F32)
    low = (rest - middle).astype(BF16).astype(F32)
    return high, middle, low


def emit_kernel(scale, returned_ref, *refs):
    *shared_refs, observer_ref, signal_ref = refs
    members = len(shared_refs)
    panels = shared_refs[0].shape[1]
    ox, oy, oz = observer_ref[0:1, :], observer_ref[1:2, :], observer_ref[2:3, :]
    none = jnp.zeros_like(ox)
    features = jnp.concatenate(
        [ox, oy, oz, none + 1.0, ox * ox + oy * oy + oz * oz, none, none, none], axis=0
    )
    h, m, w = thirds(features)
    seen = jnp.transpose(jnp.concatenate([h, m, h, m, w, h], axis=0)).astype(BF16)

    table = thirds(
        jnp.concatenate([jnp.transpose(returned_ref[:, c, :]) for c in range(4)], axis=0)
    )
    device = lax.broadcasted_iota(jnp.int32, (128, panels), 0).astype(F32)
    place = lax.broadcasted_iota(jnp.int32, (CAP, panels), 0).astype(F32)
    level = lax.broadcasted_iota(jnp.int32, (BINS, panels), 0).astype(F32)
    zero = jnp.zeros((1, panels), F32)
    for member in range(members):
        shared_ref = shared_refs[member]
        mine = [
            jnp.concatenate(
                [part[c * 128 + member * CAP :][:CAP] for c in range(4)],
                axis=0,
            )
            for part in table
        ]
        rows = jnp.concatenate(mine, axis=1).astype(BF16)
        hot = jnp.where(device == shared_ref[8:9, :], 1.0, 0.0).astype(BF16)
        looked = dot(rows, jnp.concatenate([hot, hot, hot], axis=0), NN)
        here = place == shared_ref[9:10, :]
        area = shared_ref[7:8, :] * scale
        s = [
            area
            * jnp.sum(jnp.where(here, looked[c * CAP : (c + 1) * CAP], 0.0), axis=0, keepdims=True)
            for c in range(4)
        ]
        px, py, pz = (shared_ref[k : k + 1, :] for k in (4, 5, 6))
        along = jnp.concatenate(
            [s[1], s[2], s[3], -(s[1] * px + s[2] * py + s[3] * pz), zero, zero, zero, zero], axis=0
        )
        square = jnp.concatenate(
            [-2.0 * px, -2.0 * py, -2.0 * pz, px * px + py * py + pz * pz, zero + 1.0, zero, zero, zero],
            axis=0,
        )
        h, m, w = thirds(along)
        along = dot(seen, jnp.concatenate([h, h, m, m, h, w], axis=0).astype(BF16), NN)
        h, m, w = thirds(square)
        square = dot(seen, jnp.concatenate([h, h, m, m, h, w], axis=0).astype(BF16), NN)
        inverse = lax.rsqrt(square)
        emitted = ((along * inverse + s[0]) * inverse).astype(BF16)
        for b in range(4):
            span = slice(b * OB, (b + 1) * OB)
            hot = jnp.where(shared_ref[b : b + 1, :] == level, 1.0, 0.0).astype(BF16)
            term = dot(emitted[span], hot, NT)
            signal_ref[span, :] = term if member == 0 else signal_ref[span, :] + term


def rim_kernel(fields_ref, velocity_ref, left_ref, right_ref, head_ref, tail_ref):
    for c in range(4):
        for x in range(-2, 6):
            column = column_of(fields_ref, left_ref, right_ref, c, x)
            head_ref[8 * c + x + 2] = column[0:4]
            tail_ref[8 * c + x + 2] = column[4:8]
    for k in range(3):
        for half in range(2):
            one, two = velocity_ref[k, 2 * half], velocity_ref[k, 2 * half + 1]
            head_ref[32 + 2 * k + half] = jnp.concatenate([one[0:2], two[0:2]], axis=0)
            tail_ref[32 + 2 * k + half] = jnp.concatenate([one[6:8], two[6:8]], axis=0)


def column_of(fields_ref, left_ref, right_ref, c, x):
    if x < 0:
        return left_ref[4 * c + x + 4]
    if x >= 4:
        return right_ref[4 * c + x - 4]
    return fields_ref[c, x]


def rate(center, across, tall, velocity, diffusion):
    rows, width = center.shape
    near = [
        (across[2], across[1]),
        (tall[3 : 3 + rows], tall[1 : 1 + rows]),
        (pltpu.roll(center, width - 1, 1), pltpu.roll(center, 1, 1)),
    ]
    far = [
        (across[3], across[0]),
        (tall[4 : 4 + rows], tall[0:rows]),
        (pltpu.roll(center, width - 2, 1), pltpu.roll(center, 2, 1)),
    ]
    advect = 0.0
    spread = -90.0 * center
    for k in range(3):
        advect = advect + velocity[k] * (
            8.0 * (near[k][0] - near[k][1]) - (far[k][0] - far[k][1])
        )
        spread = spread + (16.0 * (near[k][0] + near[k][1]) - (far[k][0] + far[k][1]))
    return (diffusion * spread - advect) * (1.0 / 12.0)


def transport_kernel(
    diffusion_ref, fields_ref, velocity_ref, left_ref, right_ref, low_ref, high_ref, out_ref
):
    for c in range(4):
        diffusion = diffusion_ref[c]

        def column(x):
            return column_of(fields_ref, left_ref, right_ref, c, x)

        tall = {
            x: jnp.concatenate(
                [low_ref[8 * c + x + 2][2:4], column(x), high_ref[8 * c + x + 2][0:2]], axis=0
            )
            for x in range(-2, 6)
        }
        middle = {}
        taller = {}
        for x in range(4):
            center = tall[x]
            wide = jnp.concatenate(
                [low_ref[8 * c + x + 2][0:2], center, high_ref[8 * c + x + 2][2:4]], axis=0
            )
            velocity = []
            for k in range(3):
                spot, part = 32 + 2 * k + x // 2, slice(2 * (x % 2), 2 * (x % 2) + 2)
                velocity.append(
                    jnp.concatenate(
                        [low_ref[spot][part], velocity_ref[k, x], high_ref[spot][part]], axis=0
                    )
                )
            across = [tall[x + d] for d in (-2, -1, 1, 2)]
            taller[x] = center + TIME_STEP * rate(center, across, wide, velocity, diffusion)
            middle[x] = taller[x][2:10]
        for x in (-2, -1, 4, 5):
            center = column(x)
            side, spot = (left_ref, x + 2) if x < 0 else (right_ref, x - 4)
            velocity = [side[16 + 2 * k + spot] for k in range(3)]
            across = [column(x + d) for d in (-2, -1, 1, 2)]
            middle[x] = center + TIME_STEP * rate(center, across, tall[x], velocity, diffusion)
        for x in range(4):
            velocity = [velocity_ref[k, x] for k in range(3)]
            across = [middle[x + d] for d in (-2, -1, 1, 2)]
            change = rate(middle[x], across, taller[x], velocity, diffusion)
            out_ref[c, x] = 0.5 * fields_ref[c, x] + 0.5 * (middle[x] + TIME_STEP * change)


def neighbours(axis, count, head, tail):
    return (
        lax.ppermute(tail, axis, [(i, (i + 1) % count) for i in range(count)]),
        lax.ppermute(head, axis, [((i + 1) % count, i) for i in range(count)]),
    )


def exchange(array, axes):
    return lax.all_to_all(array, axes, split_axis=0, concat_axis=0, tiled=True)


VM = pl.BlockSpec(memory_space=pltpu.VMEM)
ANY = pl.BlockSpec(memory_space=pl.ANY)
SM = pl.BlockSpec(memory_space=pltpu.SMEM)


def call(kernel, outs, in_specs, args, name, flops, moved, limit=VMEM_LIMIT):
    return pl.pallas_call(
        kernel,
        out_shape=outs,
        in_specs=in_specs,
        out_specs=jax.tree.map(lambda _: VM, outs),
        compiler_params=pltpu.CompilerParams(vmem_limit_bytes=limit),
        cost_estimate=pl.CostEstimate(flops=flops, bytes_accessed=moved, transcendentals=0),
        name=name,
    )(*args)


def ask(owner, cell):
    panels = owner.shape[1]
    return pl.pallas_call(
        ask_kernel,
        out_shape=(
            jax.ShapeDtypeStruct((128, 128), jnp.int32),
            jax.ShapeDtypeStruct((8, panels), F32),
        ),
        in_specs=[ANY, ANY],
        out_specs=(VM, VM),
        scratch_shapes=[
            pltpu.VMEM((1, panels), jnp.int32),
            pltpu.VMEM((1, panels), jnp.int32),
            pltpu.SemaphoreType.DMA((2,)),
        ],
        cost_estimate=pl.CostEstimate(flops=2_000_000, bytes_accessed=100_000, transcendentals=0),
        compiler_params=pltpu.CompilerParams(vmem_limit_bytes=FULL_VMEM),
        name="ask",
    )(owner, cell)


def sides_kernel(fields_ref, velocity_ref, head_ref, tail_ref, arrival):
    copies = []
    for out, first in ((head_ref, 0), (tail_ref, 2)):
        for c in range(4):
            copies.append((fields_ref.at[c], out.at[pl.ds(4 * c, 4)]))
        for k in range(3):
            copies.append((velocity_ref.at[k, pl.ds(first, 2)], out.at[pl.ds(16 + 2 * k, 2)]))
    copies = [
        pltpu.make_async_copy(source, target, arrival.at[i])
        for i, (source, target) in enumerate(copies)
    ]
    for copy in copies:
        copy.start()
    for copy in copies:
        copy.wait()


def make_sides(fields, velocity):
    side = jax.ShapeDtypeStruct((22, 8, 512), F32)
    return pl.pallas_call(
        sides_kernel,
        out_shape=(side, side),
        in_specs=[ANY, ANY],
        out_specs=(ANY, ANY),
        scratch_shapes=[pltpu.SemaphoreType.DMA((14,))],
        cost_estimate=pl.CostEstimate(flops=0, bytes_accessed=1_400_000, transcendentals=0),
        compiler_params=pltpu.CompilerParams(vmem_limit_bytes=FULL_VMEM),
        name="sides",
    )(fields, velocity)


def per_device(
    fields,
    velocity,
    diffusion,
    panel_owner,
    panel_cell,
    panel_bins,
    panel_position,
    panel_area,
    observer_position,
):
    shape = jax.ShapeDtypeStruct
    after = lax.optimization_barrier
    panels = panel_cell.shape[0]
    every = ("hi", "lo", "gy")
    share = shape((16, panels), F32)
    rims = shape((38, 4, 512), F32)

    requests, place = ask(panel_owner.reshape(1, panels), panel_cell.reshape(1, panels))
    arrived = exchange(requests, every)

    at = lax.axis_index("hi")
    observers = lax.dynamic_slice_in_dim(observer_position, at * 512, 512, 1)
    cells, speeds, _ = after((fields, velocity, requests))
    head, tail = make_sides(cells, speeds)
    arrived = after((arrived, head, tail))[0]
    left, right = neighbours(("hi", "lo"), 32, head, tail)
    group = call(
        pack_kernel,
        (share, share, share, share),
        [SM] + [VM] * 4,
        (
            at.reshape(1),
            after((place, head))[0],
            panel_bins,
            panel_position,
            panel_area.reshape(1, panels),
        ),
        "pack",
        100_000,
        500_000,
    )
    group = list(group)
    for k in range(1, 4):
        group[k] = lax.ppermute(group[k], "hi", [(i, (i - k) % 4) for i in range(4)])

    reply = call(
        owner_kernel,
        shape((128, 4, 128), F32),
        [VM] * 2,
        (arrived, fields),
        "sample",
        5_000_000_000,
        600_000,
    )
    returned = exchange(reply, every)

    left, right, _ = after((left, right, reply))
    head, tail = call(
        rim_kernel,
        (rims, rims),
        [VM] * 4,
        (fields, velocity, left, right),
        "rim",
        100_000,
        2_000_000,
    )
    low, high = neighbours("gy", 4, head, tail)

    scale = (BINS / (panels * 128)) ** 0.5
    partial = call(
        functools.partial(emit_kernel, scale),
        shape((512, BINS), F32),
        [VM] * 6,
        (returned, *group, observers),
        "emit",
        600_000_000,
        800_000,
    )
    parts = exchange(partial.reshape(32, 16, BINS), ("lo", "gy"))

    low, high, _ = after((low, high, partial))
    advanced = call(
        transport_kernel,
        shape(fields.shape, F32),
        [SM] + [VM] * 6,
        (diffusion, fields, velocity, left, right, low, high),
        "transport",
        16_000_000,
        3_000_000,
    )
    parts, advanced = after((parts, advanced))
    return advanced, jnp.sum(parts, axis=0)


def solution(mesh):
    count_x, count_y = mesh.devices.shape
    split = Mesh(mesh.devices.reshape(4, count_x // 4, count_y), ("hi", "lo", "gy"))
    gx = ("hi", "lo")
    every = ("hi", "lo", "gy")

    in_specs = (
        P(None, gx, "gy", None),
        P(None, gx, "gy", None),
        P(),
        P(every, None),
        P(every),
        P(None, every),
        P(None, every),
        P(every),
        P(),
    )
    out_specs = (P(None, gx, "gy", None), P(every, None))
    return jax.shard_map(
        per_device, mesh=split, in_specs=in_specs, out_specs=out_specs, check_vma=False
    )
```

```python
import functools

import jax
import jax.numpy as jnp
from jax import lax
from jax.experimental import pallas as pl
from jax.experimental.pallas import tpu as pltpu
from jax.sharding import Mesh
from jax.sharding import PartitionSpec as P

OBS = 2048
BINS = 128
OB = 128
CAP = 32
TIME_STEP = 0.15
VMEM_LIMIT = 48 * 1024 * 1024
FULL_VMEM = 60 * 1024 * 1024
F32 = jnp.float32
BF16 = jnp.bfloat16
NT = (((1,), (1,)), ((), ()))
NN = (((1,), (0,)), ((), ()))


def dot(a, b, dims):
    return lax.dot_general(a, b, dims, preferred_element_type=F32)


def ask_kernel(
    owner_in,
    cell_in,
    bins_in,
    position_in,
    area_in,
    fields_in,
    velocity_in,
    request_ref,
    share_ref,
    head_ref,
    tail_ref,
    owner_ref,
    cell_ref,
    bins_ref,
    position_ref,
    area_ref,
    arrival,
):
    pairs = [
        (owner_in, owner_ref),
        (cell_in, cell_ref),
        (bins_in, bins_ref),
        (position_in, position_ref),
        (area_in, area_ref),
    ]
    for out, first in ((head_ref, 0), (tail_ref, 2)):
        for c in range(4):
            pairs.append((fields_in.at[c], out.at[pl.ds(4 * c, 4)]))
        for k in range(3):
            pairs.append((velocity_in.at[k, pl.ds(first, 2)], out.at[pl.ds(16 + 2 * k, 2)]))
    loads = [
        pltpu.make_async_copy(source, target, arrival.at[i])
        for i, (source, target) in enumerate(pairs)
    ]
    for load in loads:
        load.start()
    panels = owner_ref.shape[1]
    chunk = 256
    ahead = lax.broadcasted_iota(jnp.int32, (chunk, 2 * chunk), 0)
    behind = lax.broadcasted_iota(jnp.int32, (chunk, 2 * chunk), 1)
    before = jnp.where((ahead < behind) | (behind >= chunk), 1.0, 0.0).astype(BF16)
    device = lax.broadcasted_iota(jnp.int32, (128, chunk), 0)
    place = device % CAP
    running = jnp.zeros((128, chunk), F32)
    table = jnp.zeros((128, 256), F32)
    for load in loads[:2]:
        load.wait()
    for k in range(panels // chunk):
        span = slice(k * chunk, (k + 1) * chunk)
        owner = owner_ref[:, span]
        cell = cell_ref[:, span]
        hit = jnp.where(device == owner, 1.0, 0.0)
        hot = hit.astype(BF16)
        counted = dot(hot, before, NN)
        rank = jnp.sum(hit * (counted[:, :chunk] + running), axis=0, keepdims=True)
        running = running + counted[:, chunk:]
        mine = place == rank.astype(jnp.int32)
        high = jnp.where(mine, (cell >> 7).astype(F32), 0.0)
        low = jnp.where(mine, (cell & 127).astype(F32), 0.0)
        table = table + dot(hot, jnp.concatenate([high, low], axis=0).astype(BF16), NT)
        share_ref[20:21, span] = owner.astype(F32)
        share_ref[21:22, span] = rank
    request_ref[...] = (table[:, :128] * 128.0 + table[:, 128:]).astype(jnp.int32)
    for load in loads[2:]:
        load.wait()
    share_ref[0:16, :] = bins_ref[...].astype(F32)
    share_ref[16:19, :] = position_ref[...]
    share_ref[19:20, :] = area_ref[...]
    share_ref[22:24, :] = jnp.zeros((2, panels), F32)


def owner_kernel(arrived_ref, fields_ref, reply_ref):
    group = lax.broadcasted_iota(jnp.int32, (32, 128), 1) // CAP
    cells = jnp.zeros((32, 128), jnp.int32)
    for member in range(4):
        cells = jnp.where(group == member, arrived_ref[member * 32 : member * 32 + 32, :], cells)
    block = cells >> 7
    key = ((cells >> 6) & 1) * 128 + ((block >> 5) * 4 + (block & 3)) * 8 + ((block >> 2) & 7)
    spot = cells & 63

    tables = []
    for c in range(4):
        rows = jnp.concatenate(
            [fields_ref[c, x, :, z * 128 : (z + 1) * 128] for x in range(4) for z in range(4)],
            axis=0,
        )
        rows = jnp.transpose(rows)
        rows = jnp.concatenate([rows[:64], rows[64:]], axis=1)
        tables.append(jnp.concatenate(thirds(rows), axis=1).astype(BF16))
    table = jnp.concatenate(tables, axis=0)

    row = lax.broadcasted_iota(jnp.int32, (256, 128), 0)
    lane = lax.broadcasted_iota(jnp.int32, (64, 128), 0)
    for g in range(0, 32, 8):
        hot = jnp.concatenate(
            [jnp.where(row == key[g + j : g + j + 1], 1.0, 0.0).astype(BF16) for j in range(8)],
            axis=1,
        )
        looked = dot(table, jnp.concatenate([hot, hot, hot], axis=0), NN)
        for j in range(8):
            mine = lane == spot[g + j : g + j + 1]
            found = jnp.concatenate(
                [
                    jnp.sum(
                        jnp.where(mine, looked[c * 64 : c * 64 + 64, j * 128 : j * 128 + 128], 0.0),
                        axis=0,
                        keepdims=True,
                    )
                    for c in range(4)
                ],
                axis=0,
            )
            for member in range(4):
                turned = found if member == 0 else pltpu.roll(found, 128 - CAP * member, 1)
                reply_ref[member * 32 + g + j] = turned


def thirds(x):
    high = x.astype(BF16).astype(F32)
    rest = x - high
    middle = rest.astype(BF16).astype(F32)
    low = (rest - middle).astype(BF16).astype(F32)
    return high, middle, low


def emit_kernel(scale, returned_ref, *refs):
    *shared_refs, at_ref, observer_ref, signal_ref = refs
    members = len(shared_refs)
    panels = shared_refs[0].shape[1]
    at = at_ref[0]
    observers = observer_ref[:, pl.ds(pl.multiple_of(at * 512, 512), 512)]
    ox, oy, oz = observers[0:1], observers[1:2], observers[2:3]
    none = jnp.zeros_like(ox)
    features = jnp.concatenate(
        [ox, oy, oz, none + 1.0, ox * ox + oy * oy + oz * oz, none, none, none], axis=0
    )
    h, m, w = thirds(features)
    seen = jnp.transpose(jnp.concatenate([h, m, h, m, w, h], axis=0)).astype(BF16)

    table = thirds(
        jnp.concatenate([jnp.transpose(returned_ref[:, c, :]) for c in range(4)], axis=0)
    )
    device = lax.broadcasted_iota(jnp.int32, (128, panels), 0).astype(F32)
    place = lax.broadcasted_iota(jnp.int32, (CAP, panels), 0).astype(F32)
    level = lax.broadcasted_iota(jnp.int32, (BINS, panels), 0).astype(F32)
    zero = jnp.zeros((1, panels), F32)
    for member in range(members):
        shared_ref = shared_refs[member]
        mine = [
            jnp.concatenate(
                [part[c * 128 + member * CAP :][:CAP] for c in range(4)],
                axis=0,
            )
            for part in table
        ]
        rows = jnp.concatenate(mine, axis=1).astype(BF16)
        hot = jnp.where(device == shared_ref[20:21, :], 1.0, 0.0).astype(BF16)
        looked = dot(rows, jnp.concatenate([hot, hot, hot], axis=0), NN)
        here = place == shared_ref[21:22, :]
        area = shared_ref[19:20, :] * scale
        s = [
            area
            * jnp.sum(jnp.where(here, looked[c * CAP : (c + 1) * CAP], 0.0), axis=0, keepdims=True)
            for c in range(4)
        ]
        px, py, pz = (shared_ref[k : k + 1, :] for k in (16, 17, 18))
        along = jnp.concatenate(
            [s[1], s[2], s[3], -(s[1] * px + s[2] * py + s[3] * pz), zero, zero, zero, zero], axis=0
        )
        square = jnp.concatenate(
            [-2.0 * px, -2.0 * py, -2.0 * pz, px * px + py * py + pz * pz, zero + 1.0, zero, zero, zero],
            axis=0,
        )
        h, m, w = thirds(along)
        along = dot(seen, jnp.concatenate([h, h, m, m, h, w], axis=0).astype(BF16), NN)
        h, m, w = thirds(square)
        square = dot(seen, jnp.concatenate([h, h, m, m, h, w], axis=0).astype(BF16), NN)
        inverse = lax.rsqrt(square)
        emitted = ((along * inverse + s[0]) * inverse).astype(BF16)
        bins = shared_ref[0:4, :]
        for k in range(1, 4):
            bins = jnp.where(at == k, shared_ref[4 * k : 4 * k + 4, :], bins)
        for b in range(4):
            span = slice(b * OB, (b + 1) * OB)
            hot = jnp.where(bins[b : b + 1] == level, 1.0, 0.0).astype(BF16)
            term = dot(emitted[span], hot, NT)
            signal_ref[span, :] = term if member == 0 else signal_ref[span, :] + term


def rim_kernel(fields_ref, velocity_ref, left_ref, right_ref, head_ref, tail_ref):
    for c in range(4):
        for x in range(-2, 6):
            column = column_of(fields_ref, left_ref, right_ref, c, x)
            head_ref[8 * c + x + 2] = column[0:4]
            tail_ref[8 * c + x + 2] = column[4:8]
    for k in range(3):
        for half in range(2):
            one, two = velocity_ref[k, 2 * half], velocity_ref[k, 2 * half + 1]
            head_ref[32 + 2 * k + half] = jnp.concatenate([one[0:2], two[0:2]], axis=0)
            tail_ref[32 + 2 * k + half] = jnp.concatenate([one[6:8], two[6:8]], axis=0)


def column_of(fields_ref, left_ref, right_ref, c, x):
    if x < 0:
        return left_ref[4 * c + x + 4]
    if x >= 4:
        return right_ref[4 * c + x - 4]
    return fields_ref[c, x]


def rate(center, across, tall, velocity, diffusion):
    rows, width = center.shape
    near = [
        (across[2], across[1]),
        (tall[3 : 3 + rows], tall[1 : 1 + rows]),
        (pltpu.roll(center, width - 1, 1), pltpu.roll(center, 1, 1)),
    ]
    far = [
        (across[3], across[0]),
        (tall[4 : 4 + rows], tall[0:rows]),
        (pltpu.roll(center, width - 2, 1), pltpu.roll(center, 2, 1)),
    ]
    advect = 0.0
    spread = -90.0 * center
    for k in range(3):
        advect = advect + velocity[k] * (
            8.0 * (near[k][0] - near[k][1]) - (far[k][0] - far[k][1])
        )
        spread = spread + (16.0 * (near[k][0] + near[k][1]) - (far[k][0] + far[k][1]))
    return (diffusion * spread - advect) * (1.0 / 12.0)


def transport_kernel(
    diffusion_ref, fields_ref, velocity_ref, left_ref, right_ref, low_ref, high_ref, out_ref
):
    for c in range(4):
        diffusion = diffusion_ref[c]

        def column(x):
            return column_of(fields_ref, left_ref, right_ref, c, x)

        tall = {
            x: jnp.concatenate(
                [low_ref[8 * c + x + 2][2:4], column(x), high_ref[8 * c + x + 2][0:2]], axis=0
            )
            for x in range(-2, 6)
        }
        middle = {}
        taller = {}
        for x in range(4):
            center = tall[x]
            wide = jnp.concatenate(
                [low_ref[8 * c + x + 2][0:2], center, high_ref[8 * c + x + 2][2:4]], axis=0
            )
            velocity = []
            for k in range(3):
                spot, part = 32 + 2 * k + x // 2, slice(2 * (x % 2), 2 * (x % 2) + 2)
                velocity.append(
                    jnp.concatenate(
                        [low_ref[spot][part], velocity_ref[k, x], high_ref[spot][part]], axis=0
                    )
                )
            across = [tall[x + d] for d in (-2, -1, 1, 2)]
            taller[x] = center + TIME_STEP * rate(center, across, wide, velocity, diffusion)
            middle[x] = taller[x][2:10]
        for x in (-2, -1, 4, 5):
            center = column(x)
            side, spot = (left_ref, x + 2) if x < 0 else (right_ref, x - 4)
            velocity = [side[16 + 2 * k + spot] for k in range(3)]
            across = [column(x + d) for d in (-2, -1, 1, 2)]
            middle[x] = center + TIME_STEP * rate(center, across, tall[x], velocity, diffusion)
        for x in range(4):
            velocity = [velocity_ref[k, x] for k in range(3)]
            across = [middle[x + d] for d in (-2, -1, 1, 2)]
            change = rate(middle[x], across, taller[x], velocity, diffusion)
            out_ref[c, x] = 0.5 * fields_ref[c, x] + 0.5 * (middle[x] + TIME_STEP * change)


def neighbours(axis, count, head, tail):
    return (
        lax.ppermute(tail, axis, [(i, (i + 1) % count) for i in range(count)]),
        lax.ppermute(head, axis, [((i + 1) % count, i) for i in range(count)]),
    )


def exchange(array, axes):
    return lax.all_to_all(array, axes, split_axis=0, concat_axis=0, tiled=True)


VM = pl.BlockSpec(memory_space=pltpu.VMEM)
ANY = pl.BlockSpec(memory_space=pl.ANY)
SM = pl.BlockSpec(memory_space=pltpu.SMEM)


def call(kernel, outs, in_specs, args, name, flops, moved, limit=VMEM_LIMIT):
    return pl.pallas_call(
        kernel,
        out_shape=outs,
        in_specs=in_specs,
        out_specs=jax.tree.map(lambda _: VM, outs),
        compiler_params=pltpu.CompilerParams(vmem_limit_bytes=limit),
        cost_estimate=pl.CostEstimate(flops=flops, bytes_accessed=moved, transcendentals=0),
        name=name,
    )(*args)


def ask(owner, cell, bins, position, area, fields, velocity):
    panels = owner.shape[1]
    side = jax.ShapeDtypeStruct((22, 8, 512), F32)
    return pl.pallas_call(
        ask_kernel,
        out_shape=(
            jax.ShapeDtypeStruct((128, 128), jnp.int32),
            jax.ShapeDtypeStruct((24, panels), F32),
            side,
            side,
        ),
        in_specs=[ANY] * 7,
        out_specs=(VM, VM, VM, VM),
        scratch_shapes=[
            pltpu.VMEM((1, panels), jnp.int32),
            pltpu.VMEM((1, panels), jnp.int32),
            pltpu.VMEM((16, panels), jnp.int32),
            pltpu.VMEM((3, panels), F32),
            pltpu.VMEM((1, panels), F32),
            pltpu.SemaphoreType.DMA((19,)),
        ],
        cost_estimate=pl.CostEstimate(flops=2_000_000, bytes_accessed=100_000, transcendentals=0),
        compiler_params=pltpu.CompilerParams(vmem_limit_bytes=FULL_VMEM),
        name="ask",
    )(owner, cell, bins, position, area, fields, velocity)


def per_device(
    fields,
    velocity,
    diffusion,
    panel_owner,
    panel_cell,
    panel_bins,
    panel_position,
    panel_area,
    observer_position,
):
    shape = jax.ShapeDtypeStruct
    after = lax.optimization_barrier
    panels = panel_cell.shape[0]
    every = ("hi", "lo", "gy")
    rims = shape((38, 4, 512), F32)

    requests, share, head, tail = ask(
        panel_owner.reshape(1, panels),
        panel_cell.reshape(1, panels),
        panel_bins,
        panel_position,
        panel_area.reshape(1, panels),
        fields,
        velocity,
    )
    arrived = exchange(requests, every)

    left, right = neighbours(("hi", "lo"), 32, head, tail)
    group = [share]
    for k in range(1, 4):
        group.append(lax.ppermute(share, "hi", [(i, (i - k) % 4) for i in range(4)]))
    at = lax.axis_index("hi").reshape(1)

    reply = call(
        owner_kernel,
        shape((128, 4, 128), F32),
        [VM] * 2,
        (arrived, fields),
        "sample",
        5_000_000_000,
        600_000,
    )
    returned = exchange(reply, every)

    left, right, _ = after((left, right, reply))
    head, tail = call(
        rim_kernel,
        (rims, rims),
        [VM] * 4,
        (fields, velocity, left, right),
        "rim",
        100_000,
        2_000_000,
    )
    low, high = neighbours("gy", 4, head, tail)

    scale = (BINS / (panels * 128)) ** 0.5
    partial = call(
        functools.partial(emit_kernel, scale),
        shape((512, BINS), F32),
        [VM] * 5 + [SM, VM],
        (returned, *group, at, observer_position),
        "emit",
        600_000_000,
        800_000,
    )
    parts = exchange(partial.reshape(32, 16, BINS), ("lo", "gy"))

    low, high, _ = after((low, high, partial))
    advanced = call(
        transport_kernel,
        shape(fields.shape, F32),
        [SM] + [VM] * 6,
        (diffusion, fields, velocity, left, right, low, high),
        "transport",
        16_000_000,
        3_000_000,
    )
    parts, advanced = after((parts, advanced))
    return advanced, jnp.sum(parts, axis=0)


def solution(mesh):
    count_x, count_y = mesh.devices.shape
    split = Mesh(mesh.devices.reshape(4, count_x // 4, count_y), ("hi", "lo", "gy"))
    gx = ("hi", "lo")
    every = ("hi", "lo", "gy")

    in_specs = (
        P(None, gx, "gy", None),
        P(None, gx, "gy", None),
        P(),
        P(every, None),
        P(every),
        P(None, every),
        P(None, every),
        P(every),
        P(),
    )
    out_specs = (P(None, gx, "gy", None), P(every, None))
    return jax.shard_map(
        per_device, mesh=split, in_specs=in_specs, out_specs=out_specs, check_vma=False
    )
```

```python
import functools

import jax
import jax.numpy as jnp
from jax import lax
from jax.experimental import pallas as pl
from jax.experimental.pallas import tpu as pltpu
from jax.sharding import Mesh
from jax.sharding import PartitionSpec as P

OBS = 2048
BINS = 128
OB = 128
CAP = 32
GX = ("zh", "zl", "xh", "xl", "yl")
TIME_STEP = 0.15
VMEM_LIMIT = 48 * 1024 * 1024
FULL_VMEM = 60 * 1024 * 1024
F32 = jnp.float32
BF16 = jnp.bfloat16
NT = (((1,), (1,)), ((), ()))
NN = (((1,), (0,)), ((), ()))


def dot(a, b, dims):
    return lax.dot_general(a, b, dims, preferred_element_type=F32)


def ask_kernel(
    owner_in,
    cell_in,
    bins_in,
    position_in,
    area_in,
    fields_in,
    velocity_in,
    request_ref,
    share_ref,
    head_ref,
    tail_ref,
    owner_ref,
    cell_ref,
    bins_ref,
    position_ref,
    area_ref,
    arrival,
):
    pairs = [
        (owner_in, owner_ref),
        (cell_in, cell_ref),
        (bins_in, bins_ref),
        (position_in, position_ref),
        (area_in, area_ref),
    ]
    for out, first in ((head_ref, 0), (tail_ref, 2)):
        for c in range(4):
            pairs.append((fields_in.at[c], out.at[pl.ds(4 * c, 4)]))
        for k in range(3):
            pairs.append((velocity_in.at[k, pl.ds(first, 2)], out.at[pl.ds(16 + 2 * k, 2)]))
    loads = [
        pltpu.make_async_copy(source, target, arrival.at[i])
        for i, (source, target) in enumerate(pairs)
    ]
    for load in loads:
        load.start()
    panels = owner_ref.shape[1]
    chunk = 256
    ahead = lax.broadcasted_iota(jnp.int32, (chunk, 2 * chunk), 0)
    behind = lax.broadcasted_iota(jnp.int32, (chunk, 2 * chunk), 1)
    before = jnp.where((ahead < behind) | (behind >= chunk), 1.0, 0.0).astype(BF16)
    device = lax.broadcasted_iota(jnp.int32, (128, chunk), 0)
    place = device % CAP
    running = jnp.zeros((128, chunk), F32)
    table = jnp.zeros((128, 256), F32)
    for load in loads[:2]:
        load.wait()
    for k in range(panels // chunk):
        span = slice(k * chunk, (k + 1) * chunk)
        owner = owner_ref[:, span]
        cell = cell_ref[:, span]
        hit = jnp.where(device == owner, 1.0, 0.0)
        hot = hit.astype(BF16)
        counted = dot(hot, before, NN)
        rank = jnp.sum(hit * (counted[:, :chunk] + running), axis=0, keepdims=True)
        running = running + counted[:, chunk:]
        mine = place == rank.astype(jnp.int32)
        high = jnp.where(mine, (cell >> 7).astype(F32), 0.0)
        low = jnp.where(mine, (cell & 127).astype(F32), 0.0)
        table = table + dot(hot, jnp.concatenate([high, low], axis=0).astype(BF16), NT)
        share_ref[20:21, span] = owner.astype(F32)
        share_ref[21:22, span] = rank
    request_ref[...] = (table[:, :128] * 128.0 + table[:, 128:]).astype(jnp.int32)
    for load in loads[2:]:
        load.wait()
    share_ref[0:16, :] = bins_ref[...].astype(F32)
    share_ref[16:19, :] = position_ref[...]
    share_ref[19:20, :] = area_ref[...]
    share_ref[22:24, :] = jnp.zeros((2, panels), F32)


def owner_kernel(arrived_ref, fields_ref, reply_ref):
    group = lax.broadcasted_iota(jnp.int32, (8, 128), 1) // CAP
    first = [[64 * (j // 2) + 16 * (j % 2) + 32 * (m // 2) + 8 * (m % 2) for m in range(4)] for j in range(4)]
    cells = []
    for j in range(4):
        eight = jnp.zeros((8, 128), jnp.int32)
        for member in range(4):
            start = first[j][member]
            eight = jnp.where(group == member, arrived_ref[start : start + 8, :], eight)
        cells.append(eight)
    cells = jnp.concatenate(cells, axis=0)
    even = (lax.broadcasted_iota(jnp.int32, (4, 128), 1) // CAP) % 2 == 0
    block = cells >> 7
    key = ((cells >> 6) & 1) * 128 + ((block >> 5) * 4 + (block & 3)) * 8 + ((block >> 2) & 7)
    spot = cells & 63

    tables = []
    for c in range(4):
        rows = jnp.concatenate(
            [fields_ref[c, x, :, z * 128 : (z + 1) * 128] for x in range(4) for z in range(4)],
            axis=0,
        )
        rows = jnp.transpose(rows)
        rows = jnp.concatenate([rows[:64], rows[64:]], axis=1)
        tables.append(jnp.concatenate(thirds(rows), axis=1).astype(BF16))
    table = jnp.concatenate(tables, axis=0)

    row = lax.broadcasted_iota(jnp.int32, (256, 128), 0)
    lane = lax.broadcasted_iota(jnp.int32, (64, 128), 0)
    for g in range(0, 32, 8):
        hot = jnp.concatenate(
            [jnp.where(row == key[g + j : g + j + 1], 1.0, 0.0).astype(BF16) for j in range(8)],
            axis=1,
        )
        looked = dot(table, jnp.concatenate([hot, hot, hot], axis=0), NN)
        for j in range(8):
            mine = lane == spot[g + j : g + j + 1]
            found = jnp.concatenate(
                [
                    jnp.sum(
                        jnp.where(mine, looked[c * 64 : c * 64 + 64, j * 128 : j * 128 + 128], 0.0),
                        axis=0,
                        keepdims=True,
                    )
                    for c in range(4)
                ],
                axis=0,
            )
            swapped = jnp.where(
                even, pltpu.roll(found, 128 - CAP, 1), pltpu.roll(found, CAP, 1)
            )
            turned = [found, swapped, pltpu.roll(found, 64, 1), pltpu.roll(swapped, 64, 1)]
            for member in range(4):
                reply_ref[first[g // 8][member] + j] = turned[member]


def thirds(x):
    high = x.astype(BF16).astype(F32)
    rest = x - high
    middle = rest.astype(BF16).astype(F32)
    low = (rest - middle).astype(BF16).astype(F32)
    return high, middle, low


def emit_kernel(scale, returned_ref, *refs):
    *shared_refs, at_ref, observer_ref, signal_ref = refs
    members = len(shared_refs)
    panels = shared_refs[0].shape[1]
    at = at_ref[0]
    blocks = (0, 2, 8, 10)
    observers = jnp.concatenate(
        [observer_ref[:, pl.ds(pl.multiple_of((at + k) * OB, OB), OB)] for k in blocks], axis=1
    )
    ox, oy, oz = observers[0:1], observers[1:2], observers[2:3]
    none = jnp.zeros_like(ox)
    features = jnp.concatenate(
        [ox, oy, oz, none + 1.0, ox * ox + oy * oy + oz * oz, none, none, none], axis=0
    )
    h, m, w = thirds(features)
    seen = jnp.transpose(jnp.concatenate([h, m, h, m, w, h], axis=0)).astype(BF16)

    table = thirds(
        jnp.concatenate([jnp.transpose(returned_ref[:, c, :]) for c in range(4)], axis=0)
    )
    device = lax.broadcasted_iota(jnp.int32, (128, panels), 0).astype(F32)
    place = lax.broadcasted_iota(jnp.int32, (CAP, panels), 0).astype(F32)
    level = lax.broadcasted_iota(jnp.int32, (BINS, panels), 0).astype(F32)
    zero = jnp.zeros((1, panels), F32)
    total = [None] * 4
    for member in range(members):
        shared_ref = shared_refs[member]
        mine = [
            jnp.concatenate(
                [part[c * 128 + member * CAP :][:CAP] for c in range(4)],
                axis=0,
            )
            for part in table
        ]
        rows = jnp.concatenate(mine, axis=1).astype(BF16)
        hot = jnp.where(device == shared_ref[20:21, :], 1.0, 0.0).astype(BF16)
        looked = dot(rows, jnp.concatenate([hot, hot, hot], axis=0), NN)
        here = place == shared_ref[21:22, :]
        area = shared_ref[19:20, :] * scale
        s = [
            area
            * jnp.sum(jnp.where(here, looked[c * CAP : (c + 1) * CAP], 0.0), axis=0, keepdims=True)
            for c in range(4)
        ]
        px, py, pz = (shared_ref[k : k + 1, :] for k in (16, 17, 18))
        along = jnp.concatenate(
            [s[1], s[2], s[3], -(s[1] * px + s[2] * py + s[3] * pz), zero, zero, zero, zero], axis=0
        )
        square = jnp.concatenate(
            [-2.0 * px, -2.0 * py, -2.0 * pz, px * px + py * py + pz * pz, zero + 1.0, zero, zero, zero],
            axis=0,
        )
        h, m, w = thirds(along)
        along = dot(seen, jnp.concatenate([h, h, m, m, h, w], axis=0).astype(BF16), NN)
        h, m, w = thirds(square)
        square = dot(seen, jnp.concatenate([h, h, m, m, h, w], axis=0).astype(BF16), NN)
        inverse = lax.rsqrt(square)
        emitted = ((along * inverse + s[0]) * inverse).astype(BF16)
        for b in range(4):
            bins = shared_ref[blocks[b] : blocks[b] + 1, :]
            for k in (1, 4, 5):
                bins = jnp.where(at == k, shared_ref[blocks[b] + k : blocks[b] + k + 1, :], bins)
            hot = jnp.where(bins == level, 1.0, 0.0).astype(BF16)
            term = dot(emitted[b * OB : (b + 1) * OB], hot, NT)
            total[b] = term if member == 0 else total[b] + term
    for b in range(4):
        signal_ref[b * OB : (b + 1) * OB, :] = total[b]


def rim_kernel(fields_ref, velocity_ref, left_ref, right_ref, head_ref, tail_ref):
    for c in range(4):
        for x in range(-2, 6):
            column = column_of(fields_ref, left_ref, right_ref, c, x)
            head_ref[8 * c + x + 2] = column[0:4]
            tail_ref[8 * c + x + 2] = column[4:8]
    for k in range(3):
        for half in range(2):
            one, two = velocity_ref[k, 2 * half], velocity_ref[k, 2 * half + 1]
            head_ref[32 + 2 * k + half] = jnp.concatenate([one[0:2], two[0:2]], axis=0)
            tail_ref[32 + 2 * k + half] = jnp.concatenate([one[6:8], two[6:8]], axis=0)


def column_of(fields_ref, left_ref, right_ref, c, x):
    if x < 0:
        return left_ref[4 * c + x + 4]
    if x >= 4:
        return right_ref[4 * c + x - 4]
    return fields_ref[c, x]


def rate(center, across, tall, velocity, diffusion):
    rows, width = center.shape
    near = [
        (across[2], across[1]),
        (tall[3 : 3 + rows], tall[1 : 1 + rows]),
        (pltpu.roll(center, width - 1, 1), pltpu.roll(center, 1, 1)),
    ]
    far = [
        (across[3], across[0]),
        (tall[4 : 4 + rows], tall[0:rows]),
        (pltpu.roll(center, width - 2, 1), pltpu.roll(center, 2, 1)),
    ]
    advect = 0.0
    spread = -90.0 * center
    for k in range(3):
        advect = advect + velocity[k] * (
            8.0 * (near[k][0] - near[k][1]) - (far[k][0] - far[k][1])
        )
        spread = spread + (16.0 * (near[k][0] + near[k][1]) - (far[k][0] + far[k][1]))
    return (diffusion * spread - advect) * (1.0 / 12.0)


def transport_kernel(
    diffusion_ref, fields_ref, velocity_ref, left_ref, right_ref, low_ref, high_ref, out_ref
):
    for c in range(4):
        diffusion = diffusion_ref[c]

        def column(x):
            return column_of(fields_ref, left_ref, right_ref, c, x)

        tall = {
            x: jnp.concatenate(
                [low_ref[8 * c + x + 2][2:4], column(x), high_ref[8 * c + x + 2][0:2]], axis=0
            )
            for x in range(-2, 6)
        }
        middle = {}
        taller = {}
        for x in range(4):
            center = tall[x]
            wide = jnp.concatenate(
                [low_ref[8 * c + x + 2][0:2], center, high_ref[8 * c + x + 2][2:4]], axis=0
            )
            velocity = []
            for k in range(3):
                spot, part = 32 + 2 * k + x // 2, slice(2 * (x % 2), 2 * (x % 2) + 2)
                velocity.append(
                    jnp.concatenate(
                        [low_ref[spot][part], velocity_ref[k, x], high_ref[spot][part]], axis=0
                    )
                )
            across = [tall[x + d] for d in (-2, -1, 1, 2)]
            taller[x] = center + TIME_STEP * rate(center, across, wide, velocity, diffusion)
            middle[x] = taller[x][2:10]
        for x in (-2, -1, 4, 5):
            center = column(x)
            side, spot = (left_ref, x + 2) if x < 0 else (right_ref, x - 4)
            velocity = [side[16 + 2 * k + spot] for k in range(3)]
            across = [column(x + d) for d in (-2, -1, 1, 2)]
            middle[x] = center + TIME_STEP * rate(center, across, tall[x], velocity, diffusion)
        for x in range(4):
            velocity = [velocity_ref[k, x] for k in range(3)]
            across = [middle[x + d] for d in (-2, -1, 1, 2)]
            change = rate(middle[x], across, taller[x], velocity, diffusion)
            out_ref[c, x] = 0.5 * fields_ref[c, x] + 0.5 * (middle[x] + TIME_STEP * change)


def neighbours(axis, count, head, tail):
    return (
        lax.ppermute(tail, axis, [(i, (i + 1) % count) for i in range(count)]),
        lax.ppermute(head, axis, [((i + 1) % count, i) for i in range(count)]),
    )


def exchange(array, axes):
    return lax.all_to_all(array, axes, split_axis=0, concat_axis=0, tiled=True)


VM = pl.BlockSpec(memory_space=pltpu.VMEM)
ANY = pl.BlockSpec(memory_space=pl.ANY)
SM = pl.BlockSpec(memory_space=pltpu.SMEM)


def call(kernel, outs, in_specs, args, name, flops, moved, limit=VMEM_LIMIT):
    return pl.pallas_call(
        kernel,
        out_shape=outs,
        in_specs=in_specs,
        out_specs=jax.tree.map(lambda _: VM, outs),
        compiler_params=pltpu.CompilerParams(vmem_limit_bytes=limit),
        cost_estimate=pl.CostEstimate(flops=flops, bytes_accessed=moved, transcendentals=0),
        name=name,
    )(*args)


def ask(owner, cell, bins, position, area, fields, velocity):
    panels = owner.shape[1]
    side = jax.ShapeDtypeStruct((22, 8, 512), F32)
    return pl.pallas_call(
        ask_kernel,
        out_shape=(
            jax.ShapeDtypeStruct((128, 128), jnp.int32),
            jax.ShapeDtypeStruct((24, panels), F32),
            side,
            side,
        ),
        in_specs=[ANY] * 7,
        out_specs=(VM, VM, VM, VM),
        scratch_shapes=[
            pltpu.VMEM((1, panels), jnp.int32),
            pltpu.VMEM((1, panels), jnp.int32),
            pltpu.VMEM((16, panels), jnp.int32),
            pltpu.VMEM((3, panels), F32),
            pltpu.VMEM((1, panels), F32),
            pltpu.SemaphoreType.DMA((19,)),
        ],
        cost_estimate=pl.CostEstimate(flops=2_000_000, bytes_accessed=100_000, transcendentals=0),
        compiler_params=pltpu.CompilerParams(vmem_limit_bytes=FULL_VMEM),
        name="ask",
    )(owner, cell, bins, position, area, fields, velocity)


def per_device(
    fields,
    velocity,
    diffusion,
    panel_owner,
    panel_cell,
    panel_bins,
    panel_position,
    panel_area,
    observer_position,
):
    shape = jax.ShapeDtypeStruct
    after = lax.optimization_barrier
    panels = panel_cell.shape[0]
    every = (*GX, "gy")
    rims = shape((38, 4, 512), F32)

    requests, share, head, tail = ask(
        panel_owner.reshape(1, panels),
        panel_cell.reshape(1, panels),
        panel_bins,
        panel_position,
        panel_area.reshape(1, panels),
        fields,
        velocity,
    )
    arrived = exchange(requests, every)

    left, right = neighbours(GX, 32, head, tail)
    pair = [(0, 1), (1, 0)]
    beside = lax.ppermute(share, "zl", pair)
    group = [share, lax.ppermute(share, "xl", pair), beside, lax.ppermute(beside, "xl", pair)]
    at = (4 * lax.axis_index("zl") + lax.axis_index("xl")).reshape(1)

    reply = call(
        owner_kernel,
        shape((128, 4, 128), F32),
        [VM] * 2,
        (arrived, fields),
        "sample",
        5_000_000_000,
        600_000,
    )
    returned = exchange(reply, every)

    left, right, _ = after((left, right, reply))
    head, tail = call(
        rim_kernel,
        (rims, rims),
        [VM] * 4,
        (fields, velocity, left, right),
        "rim",
        100_000,
        2_000_000,
    )
    low, high = neighbours("gy", 4, head, tail)

    scale = (BINS / (panels * 128)) ** 0.5
    partial = call(
        functools.partial(emit_kernel, scale),
        shape((512, BINS), F32),
        [VM] * 5 + [SM, VM],
        (returned, *group, at, observer_position),
        "emit",
        600_000_000,
        800_000,
    )
    parts = exchange(partial.reshape(32, 16, BINS), ("zh", "xh", "yl", "gy"))

    low, high, _ = after((low, high, partial))
    advanced = call(
        transport_kernel,
        shape(fields.shape, F32),
        [SM] + [VM] * 6,
        (diffusion, fields, velocity, left, right, low, high),
        "transport",
        16_000_000,
        3_000_000,
    )
    parts, advanced = after((parts, advanced))
    return advanced, jnp.sum(parts, axis=0)


def solution(mesh):
    split = Mesh(mesh.devices.reshape(2, 2, 2, 2, 2, 4), (*GX, "gy"))
    gx, every = GX, (*GX, "gy")
    in_specs = (
        P(None, gx, "gy", None),
        P(None, gx, "gy", None),
        P(),
        P(every, None),
        P(every),
        P(None, every),
        P(None, every),
        P(every),
        P(),
    )
    out_specs = (P(None, gx, "gy", None), P(every, None))
    return jax.shard_map(
        per_device, mesh=split, in_specs=in_specs, out_specs=out_specs, check_vma=False
    )
```

```python
import functools

import jax
import jax.numpy as jnp
from jax import lax
from jax.experimental import pallas as pl
from jax.experimental.pallas import tpu as pltpu
from jax.sharding import Mesh
from jax.sharding import PartitionSpec as P

OBS = 2048
BINS = 128
OB = 128
CAP = 32
TIME_STEP = 0.15
VMEM_LIMIT = 48 * 1024 * 1024
FULL_VMEM = 60 * 1024 * 1024
F32 = jnp.float32
BF16 = jnp.bfloat16
NT = (((1,), (1,)), ((), ()))
NN = (((1,), (0,)), ((), ()))


def dot(a, b, dims):
    return lax.dot_general(a, b, dims, preferred_element_type=F32)


def ask_kernel(
    owner_in,
    cell_in,
    bins_in,
    position_in,
    area_in,
    fields_in,
    velocity_in,
    request_ref,
    share_ref,
    head_ref,
    tail_ref,
    owner_ref,
    cell_ref,
    bins_ref,
    position_ref,
    area_ref,
    arrival,
):
    pairs = [
        (owner_in, owner_ref),
        (cell_in, cell_ref),
        (bins_in, bins_ref),
        (position_in, position_ref),
        (area_in, area_ref),
    ]
    for out, first in ((head_ref, 0), (tail_ref, 2)):
        for c in range(4):
            pairs.append((fields_in.at[c], out.at[pl.ds(4 * c, 4)]))
        for k in range(3):
            pairs.append((velocity_in.at[k, pl.ds(first, 2)], out.at[pl.ds(16 + 2 * k, 2)]))
    loads = [
        pltpu.make_async_copy(source, target, arrival.at[i])
        for i, (source, target) in enumerate(pairs)
    ]
    for load in loads:
        load.start()
    panels = owner_ref.shape[1]
    chunk = 256
    ahead = lax.broadcasted_iota(jnp.int32, (chunk, 2 * chunk), 0)
    behind = lax.broadcasted_iota(jnp.int32, (chunk, 2 * chunk), 1)
    before = jnp.where((ahead < behind) | (behind >= chunk), 1.0, 0.0).astype(BF16)
    device = lax.broadcasted_iota(jnp.int32, (128, chunk), 0)
    place = device % CAP
    running = jnp.zeros((128, chunk), F32)
    table = jnp.zeros((128, 256), F32)
    for load in loads[:2]:
        load.wait()
    for k in range(panels // chunk):
        span = slice(k * chunk, (k + 1) * chunk)
        owner = owner_ref[:, span]
        cell = cell_ref[:, span]
        hit = jnp.where(device == owner, 1.0, 0.0)
        hot = hit.astype(BF16)
        counted = dot(hot, before, NN)
        rank = jnp.sum(hit * (counted[:, :chunk] + running), axis=0, keepdims=True)
        running = running + counted[:, chunk:]
        mine = place == rank.astype(jnp.int32)
        high = jnp.where(mine, (cell >> 7).astype(F32), 0.0)
        low = jnp.where(mine, (cell & 127).astype(F32), 0.0)
        table = table + dot(hot, jnp.concatenate([high, low], axis=0).astype(BF16), NT)
        share_ref[20:21, span] = owner.astype(F32)
        share_ref[21:22, span] = rank
    request_ref[...] = (table[:, :128] * 128.0 + table[:, 128:]).astype(jnp.int32)
    for load in loads[2:]:
        load.wait()
    share_ref[0:16, :] = bins_ref[...].astype(F32)
    share_ref[16:19, :] = position_ref[...]
    share_ref[19:20, :] = area_ref[...]
    share_ref[22:24, :] = jnp.zeros((2, panels), F32)


def pack_kernel(at_ref, share_ref, *outs):
    def fold(row):
        line = share_ref[row : row + 1, :]
        return jnp.concatenate([line[:, j * 128 : j * 128 + 128] for j in range(8)], axis=0)

    folded = [fold(row) for row in range(22)]
    for k in range(1, 4):
        to = (at_ref[0] + (4 - k)) % 4
        for b in range(4):
            rows = folded[b]
            for member in range(1, 4):
                rows = jnp.where(to == member, folded[4 * member + b], rows)
            outs[k - 1][b] = rows
        for j in range(6):
            outs[k - 1][4 + j] = folded[16 + j]


def owner_kernel(arrived_ref, fields_ref, reply_ref):
    group = lax.broadcasted_iota(jnp.int32, (32, 128), 1) // CAP
    cells = jnp.zeros((32, 128), jnp.int32)
    for member in range(4):
        cells = jnp.where(group == member, arrived_ref[member * 32 : member * 32 + 32, :], cells)
    block = cells >> 7
    key = ((cells >> 6) & 1) * 128 + ((block >> 5) * 4 + (block & 3)) * 8 + ((block >> 2) & 7)
    spot = cells & 63

    tables = []
    for c in range(4):
        rows = jnp.concatenate(
            [fields_ref[c, x, :, z * 128 : (z + 1) * 128] for x in range(4) for z in range(4)],
            axis=0,
        )
        rows = jnp.transpose(rows)
        rows = jnp.concatenate([rows[:64], rows[64:]], axis=1)
        tables.append(jnp.concatenate(thirds(rows), axis=1).astype(BF16))
    table = jnp.concatenate(tables, axis=0)

    row = lax.broadcasted_iota(jnp.int32, (256, 128), 0)
    lane = lax.broadcasted_iota(jnp.int32, (64, 128), 0)
    for g in range(0, 32, 8):
        hot = jnp.concatenate(
            [jnp.where(row == key[g + j : g + j + 1], 1.0, 0.0).astype(BF16) for j in range(8)],
            axis=1,
        )
        looked = dot(table, jnp.concatenate([hot, hot, hot], axis=0), NN)
        for j in range(8):
            mine = lane == spot[g + j : g + j + 1]
            found = jnp.concatenate(
                [
                    jnp.sum(
                        jnp.where(mine, looked[c * 64 : c * 64 + 64, j * 128 : j * 128 + 128], 0.0),
                        axis=0,
                        keepdims=True,
                    )
                    for c in range(4)
                ],
                axis=0,
            )
            for member in range(4):
                turned = found if member == 0 else pltpu.roll(found, 128 - CAP * member, 1)
                reply_ref[member * 32 + g + j] = turned


def thirds(x):
    high = x.astype(BF16).astype(F32)
    rest = x - high
    middle = rest.astype(BF16).astype(F32)
    low = (rest - middle).astype(BF16).astype(F32)
    return high, middle, low


def emit_kernel(scale, returned_ref, *refs):
    *shared_refs, at_ref, observer_ref, signal_ref = refs
    members = len(shared_refs)
    panels = shared_refs[0].shape[1]

    def unfold(ref, row):
        return jnp.concatenate([ref[row, j : j + 1, :] for j in range(8)], axis=1)

    at = at_ref[0]
    observers = observer_ref[:, pl.ds(pl.multiple_of(at * 512, 512), 512)]
    ox, oy, oz = observers[0:1], observers[1:2], observers[2:3]
    none = jnp.zeros_like(ox)
    features = jnp.concatenate(
        [ox, oy, oz, none + 1.0, ox * ox + oy * oy + oz * oz, none, none, none], axis=0
    )
    h, m, w = thirds(features)
    seen = jnp.transpose(jnp.concatenate([h, m, h, m, w, h], axis=0)).astype(BF16)

    table = thirds(
        jnp.concatenate([jnp.transpose(returned_ref[:, c, :]) for c in range(4)], axis=0)
    )[:2]
    device = lax.broadcasted_iota(jnp.int32, (128, panels), 0).astype(F32)
    place = lax.broadcasted_iota(jnp.int32, (CAP, panels), 0).astype(F32)
    level = lax.broadcasted_iota(jnp.int32, (BINS, panels), 0).astype(F32).astype(BF16)
    zero = jnp.zeros((1, panels), F32)
    one, none = jnp.ones((), BF16), jnp.zeros((), BF16)
    total = [None] * 4
    for member in range(members):
        shared_ref = shared_refs[member]
        if member == 0:
            bins = shared_ref[0:4, :]
            for k in range(1, 4):
                bins = jnp.where(at == k, shared_ref[4 * k : 4 * k + 4, :], bins)
            px, py, pz, area, owner, rank = (shared_ref[16 + j : 17 + j, :] for j in range(6))
        else:
            bins = jnp.concatenate([unfold(shared_ref, b) for b in range(4)], axis=0)
            px, py, pz, area, owner, rank = (unfold(shared_ref, 4 + j) for j in range(6))
        mine = [
            jnp.concatenate(
                [part[c * 128 + member * CAP :][:CAP] for c in range(4)],
                axis=0,
            )
            for part in table
        ]
        rows = jnp.concatenate(mine, axis=1).astype(BF16)
        hot = jnp.where(device == owner, 1.0, 0.0).astype(BF16)
        looked = dot(rows, jnp.concatenate([hot, hot], axis=0), NN)
        here = place == rank
        area = area * scale
        s = [
            area
            * jnp.sum(jnp.where(here, looked[c * CAP : (c + 1) * CAP], 0.0), axis=0, keepdims=True)
            for c in range(4)
        ]
        along = jnp.concatenate(
            [s[1], s[2], s[3], -(s[1] * px + s[2] * py + s[3] * pz), zero, zero, zero, zero], axis=0
        )
        square = jnp.concatenate(
            [-2.0 * px, -2.0 * py, -2.0 * pz, px * px + py * py + pz * pz, zero + 1.0, zero, zero, zero],
            axis=0,
        )
        h, m, w = thirds(along)
        along = dot(seen, jnp.concatenate([h, h, m, m, h, w], axis=0).astype(BF16), NN)
        h, m, w = thirds(square)
        square = dot(seen, jnp.concatenate([h, h, m, m, h, w], axis=0).astype(BF16), NN)
        inverse = lax.rsqrt(square)
        emitted = ((along * inverse + s[0]) * inverse).astype(BF16)
        bins = bins.astype(BF16)
        for b in range(4):
            span = slice(b * OB, (b + 1) * OB)
            hot = jnp.where(bins[b : b + 1] == level, one, none)
            term = dot(emitted[span], hot, NT)
            total[b] = term if member == 0 else total[b] + term
    for b in range(4):
        signal_ref[b * OB : (b + 1) * OB, :] = total[b]


def rim_kernel(odd_ref, fields_ref, velocity_ref, left_ref, right_ref, near_ref, far_ref):
    odd = odd_ref[0] == 1

    def put(spot, low, high):
        near_ref[spot] = jnp.where(odd, low, high)
        far_ref[spot] = jnp.where(odd, high, low)

    for c in range(4):
        for x in range(4):
            column = fields_ref[c, x]
            put(4 * c + x, column[0:4], column[4:8])
        for side in range(2):
            one, two = (
                column_of(fields_ref, left_ref, right_ref, c, x)
                for x in ((-2, -1) if side == 0 else (4, 5))
            )
            put(
                22 + 2 * c + side,
                jnp.concatenate([one[0:2], two[0:2]], axis=0),
                jnp.concatenate([one[6:8], two[6:8]], axis=0),
            )
    for k in range(3):
        for half in range(2):
            one, two = velocity_ref[k, 2 * half], velocity_ref[k, 2 * half + 1]
            put(
                16 + 2 * k + half,
                jnp.concatenate([one[0:2], two[0:2]], axis=0),
                jnp.concatenate([one[6:8], two[6:8]], axis=0),
            )


def column_of(fields_ref, left_ref, right_ref, c, x):
    if x < 0:
        return left_ref[4 * c + x + 4]
    if x >= 4:
        return right_ref[4 * c + x - 4]
    return fields_ref[c, x]


def rate(center, across, tall, velocity, diffusion):
    rows, width = center.shape
    near = [
        (across[2], across[1]),
        (tall[3 : 3 + rows], tall[1 : 1 + rows]),
        (pltpu.roll(center, width - 1, 1), pltpu.roll(center, 1, 1)),
    ]
    far = [
        (across[3], across[0]),
        (tall[4 : 4 + rows], tall[0:rows]),
        (pltpu.roll(center, width - 2, 1), pltpu.roll(center, 2, 1)),
    ]
    advect = 0.0
    spread = -90.0 * center
    for k in range(3):
        advect = advect + velocity[k] * (
            8.0 * (near[k][0] - near[k][1]) - (far[k][0] - far[k][1])
        )
        spread = spread + (16.0 * (near[k][0] + near[k][1]) - (far[k][0] + far[k][1]))
    return (diffusion * spread - advect) * (1.0 / 12.0)


def transport_kernel(
    diffusion_ref, odd_ref, fields_ref, velocity_ref, left_ref, right_ref, near_ref, far_ref, out_ref
):
    odd = odd_ref[0] == 1

    def low(spot):
        return jnp.where(odd, near_ref[spot], far_ref[spot])

    def high(spot):
        return jnp.where(odd, far_ref[spot], near_ref[spot])

    for c in range(4):
        diffusion = diffusion_ref[c]

        def column(x):
            return column_of(fields_ref, left_ref, right_ref, c, x)

        below = {x: low(4 * c + x) for x in range(4)}
        above = {x: high(4 * c + x) for x in range(4)}
        tall = {
            x: jnp.concatenate([below[x][2:4], column(x), above[x][0:2]], axis=0) for x in range(4)
        }
        for side in range(2):
            under, over = low(22 + 2 * c + side), high(22 + 2 * c + side)
            for i in range(2):
                x, part = (-2 + i, 4 + i)[side], slice(2 * i, 2 * i + 2)
                tall[x] = jnp.concatenate([under[part], column(x), over[part]], axis=0)
        middle = {}
        taller = {}
        for x in range(4):
            center = tall[x]
            wide = jnp.concatenate([below[x][0:2], center, above[x][2:4]], axis=0)
            velocity = []
            for k in range(3):
                spot, part = 16 + 2 * k + x // 2, slice(2 * (x % 2), 2 * (x % 2) + 2)
                velocity.append(
                    jnp.concatenate(
                        [low(spot)[part], velocity_ref[k, x], high(spot)[part]], axis=0
                    )
                )
            across = [tall[x + d] for d in (-2, -1, 1, 2)]
            taller[x] = center + TIME_STEP * rate(center, across, wide, velocity, diffusion)
            middle[x] = taller[x][2:10]
        for x in (-2, -1, 4, 5):
            center = column(x)
            side, spot = (left_ref, x + 2) if x < 0 else (right_ref, x - 4)
            velocity = [side[16 + 2 * k + spot] for k in range(3)]
            across = [column(x + d) for d in (-2, -1, 1, 2)]
            middle[x] = center + TIME_STEP * rate(center, across, tall[x], velocity, diffusion)
        for x in range(4):
            velocity = [velocity_ref[k, x] for k in range(3)]
            across = [middle[x + d] for d in (-2, -1, 1, 2)]
            change = rate(middle[x], across, taller[x], velocity, diffusion)
            out_ref[c, x] = 0.5 * fields_ref[c, x] + 0.5 * (middle[x] + TIME_STEP * change)


def neighbours(axis, count, head, tail):
    return (
        lax.ppermute(tail, axis, [(i, (i + 1) % count) for i in range(count)]),
        lax.ppermute(head, axis, [((i + 1) % count, i) for i in range(count)]),
    )


def exchange(array, axes):
    return lax.all_to_all(array, axes, split_axis=0, concat_axis=0, tiled=True)


VM = pl.BlockSpec(memory_space=pltpu.VMEM)
ANY = pl.BlockSpec(memory_space=pl.ANY)
SM = pl.BlockSpec(memory_space=pltpu.SMEM)


def call(kernel, outs, in_specs, args, name, flops, moved, limit=VMEM_LIMIT):
    return pl.pallas_call(
        kernel,
        out_shape=outs,
        in_specs=in_specs,
        out_specs=jax.tree.map(lambda _: VM, outs),
        compiler_params=pltpu.CompilerParams(vmem_limit_bytes=limit),
        cost_estimate=pl.CostEstimate(flops=flops, bytes_accessed=moved, transcendentals=0),
        name=name,
    )(*args)


def ask(owner, cell, bins, position, area, fields, velocity):
    panels = owner.shape[1]
    side = jax.ShapeDtypeStruct((22, 8, 512), F32)
    return pl.pallas_call(
        ask_kernel,
        out_shape=(
            jax.ShapeDtypeStruct((128, 128), jnp.int32),
            jax.ShapeDtypeStruct((24, panels), F32),
            side,
            side,
        ),
        in_specs=[ANY] * 7,
        out_specs=(VM, VM, VM, VM),
        scratch_shapes=[
            pltpu.VMEM((1, panels), jnp.int32),
            pltpu.VMEM((1, panels), jnp.int32),
            pltpu.VMEM((16, panels), jnp.int32),
            pltpu.VMEM((3, panels), F32),
            pltpu.VMEM((1, panels), F32),
            pltpu.SemaphoreType.DMA((19,)),
        ],
        cost_estimate=pl.CostEstimate(flops=2_000_000, bytes_accessed=100_000, transcendentals=0),
        compiler_params=pltpu.CompilerParams(vmem_limit_bytes=FULL_VMEM),
        name="ask",
    )(owner, cell, bins, position, area, fields, velocity)


def per_device(
    fields,
    velocity,
    diffusion,
    panel_owner,
    panel_cell,
    panel_bins,
    panel_position,
    panel_area,
    observer_position,
):
    shape = jax.ShapeDtypeStruct
    after = lax.optimization_barrier
    panels = panel_cell.shape[0]
    every = ("hi", "lo", "gy")
    rims = shape((30, 4, 512), F32)

    requests, share, head, tail = ask(
        panel_owner.reshape(1, panels),
        panel_cell.reshape(1, panels),
        panel_bins,
        panel_position,
        panel_area.reshape(1, panels),
        fields,
        velocity,
    )
    arrived = exchange(requests, every)

    left, right = neighbours(("hi", "lo"), 32, head, tail)
    at = lax.axis_index("hi").reshape(1)
    few = shape((10, 8, 128), F32)
    packed = call(
        pack_kernel,
        (few, few, few),
        [SM, VM],
        (at, share),
        "pack",
        100_000,
        250_000,
    )
    arrived = after((arrived, *packed))[0]
    group = [share]
    for k in range(1, 4):
        group.append(lax.ppermute(packed[k - 1], "hi", [(i, (i - k) % 4) for i in range(4)]))

    reply = call(
        owner_kernel,
        shape((128, 4, 128), F32),
        [VM] * 2,
        (arrived, fields),
        "sample",
        5_000_000_000,
        600_000,
    )
    returned = exchange(reply, every)

    left, right, _ = after((left, right, reply))
    odd = (lax.axis_index("gy") % 2).reshape(1)
    near, far = call(
        rim_kernel,
        (rims, rims),
        [SM] + [VM] * 4,
        (odd, fields, velocity, left, right),
        "rim",
        100_000,
        2_000_000,
    )
    returned = after((returned, near, far))[0]
    near = lax.ppermute(near, "gy", [(0, 1), (1, 0), (2, 3), (3, 2)])
    far = lax.ppermute(far, "gy", [(1, 2), (2, 1), (3, 0), (0, 3)])

    scale = (BINS / (panels * 128)) ** 0.5
    partial = call(
        functools.partial(emit_kernel, scale),
        shape((512, BINS), F32),
        [VM] * 5 + [SM, VM],
        (returned, *group, at, observer_position),
        "emit",
        5_000_000_000,
        800_000,
    )
    parts = exchange(partial.reshape(32, 16, BINS), ("lo", "gy"))

    near, far, _ = after((near, far, partial))
    advanced = call(
        transport_kernel,
        shape(fields.shape, F32),
        [SM, SM] + [VM] * 6,
        (diffusion, odd, fields, velocity, left, right, near, far),
        "transport",
        5_000_000_000,
        3_000_000,
    )
    parts, advanced = after((parts, advanced))
    return advanced, jnp.sum(parts, axis=0)


def solution(mesh):
    count_x, count_y = mesh.devices.shape
    split = Mesh(mesh.devices.reshape(4, count_x // 4, count_y), ("hi", "lo", "gy"))
    gx = ("hi", "lo")
    every = ("hi", "lo", "gy")

    in_specs = (
        P(None, gx, "gy", None),
        P(None, gx, "gy", None),
        P(),
        P(every, None),
        P(every),
        P(None, every),
        P(None, every),
        P(every),
        P(),
    )
    out_specs = (P(None, gx, "gy", None), P(every, None))
    return jax.shard_map(
        per_device, mesh=split, in_specs=in_specs, out_specs=out_specs, check_vma=False
    )
```

```python
import functools

import jax
import jax.numpy as jnp
from jax import lax
from jax.experimental import pallas as pl
from jax.experimental.pallas import tpu as pltpu
from jax.sharding import Mesh
from jax.sharding import PartitionSpec as P

OBS = 2048
BINS = 128
OB = 128
CAP = 32
TIME_STEP = 0.15
VMEM_LIMIT = 48 * 1024 * 1024
FULL_VMEM = 60 * 1024 * 1024
F32 = jnp.float32
BF16 = jnp.bfloat16
NT = (((1,), (1,)), ((), ()))
NN = (((1,), (0,)), ((), ()))


def dot(a, b, dims):
    return lax.dot_general(a, b, dims, preferred_element_type=F32)


def ask_kernel(
    owner_in,
    cell_in,
    bins_in,
    position_in,
    area_in,
    fields_in,
    velocity_in,
    request_ref,
    share_ref,
    head_ref,
    tail_ref,
    owner_ref,
    cell_ref,
    bins_ref,
    position_ref,
    area_ref,
    arrival,
):
    pairs = [
        (owner_in, owner_ref),
        (cell_in, cell_ref),
        (bins_in, bins_ref),
        (position_in, position_ref),
        (area_in, area_ref),
    ]
    for out, first in ((head_ref, 0), (tail_ref, 2)):
        for c in range(4):
            pairs.append((fields_in.at[c], out.at[pl.ds(4 * c, 4)]))
        for k in range(3):
            pairs.append((velocity_in.at[k, pl.ds(first, 2)], out.at[pl.ds(16 + 2 * k, 2)]))
    loads = [
        pltpu.make_async_copy(source, target, arrival.at[i])
        for i, (source, target) in enumerate(pairs)
    ]
    for load in loads:
        load.start()
    panels = owner_ref.shape[1]
    chunk = 256
    ahead = lax.broadcasted_iota(jnp.int32, (chunk, 2 * chunk), 0)
    behind = lax.broadcasted_iota(jnp.int32, (chunk, 2 * chunk), 1)
    before = jnp.where((ahead < behind) | (behind >= chunk), 1.0, 0.0).astype(BF16)
    device = lax.broadcasted_iota(jnp.int32, (128, chunk), 0)
    place = device % CAP
    running = jnp.zeros((128, chunk), F32)
    table = jnp.zeros((128, 256), F32)
    for load in loads[:2]:
        load.wait()
    for k in range(panels // chunk):
        span = slice(k * chunk, (k + 1) * chunk)
        owner = owner_ref[:, span]
        cell = cell_ref[:, span]
        hit = jnp.where(device == owner, 1.0, 0.0)
        hot = hit.astype(BF16)
        counted = dot(hot, before, NN)
        rank = jnp.sum(hit * (counted[:, :chunk] + running), axis=0, keepdims=True)
        running = running + counted[:, chunk:]
        mine = place == rank.astype(jnp.int32)
        high = jnp.where(mine, (cell >> 7).astype(F32), 0.0)
        low = jnp.where(mine, (cell & 127).astype(F32), 0.0)
        table = table + dot(hot, jnp.concatenate([high, low], axis=0).astype(BF16), NT)
        share_ref[20:21, span] = owner.astype(F32)
        share_ref[21:22, span] = rank
    request_ref[...] = (table[:, :128] * 128.0 + table[:, 128:]).astype(jnp.int32)
    for load in loads[2:]:
        load.wait()
    share_ref[0:16, :] = bins_ref[...].astype(F32)
    share_ref[16:19, :] = position_ref[...]
    share_ref[19:20, :] = area_ref[...]
    share_ref[22:24, :] = jnp.zeros((2, panels), F32)


def pack_kernel(at_ref, share_ref, *outs):
    def fold(row):
        line = share_ref[row : row + 1, :]
        return jnp.concatenate([line[:, j * 128 : j * 128 + 128] for j in range(8)], axis=0)

    folded = [fold(row) for row in range(22)]
    for k in range(1, 4):
        to = (at_ref[0] + (4 - k)) % 4
        for b in range(4):
            rows = folded[b]
            for member in range(1, 4):
                rows = jnp.where(to == member, folded[4 * member + b], rows)
            outs[k - 1][b] = rows
        for j in range(6):
            outs[k - 1][4 + j] = folded[16 + j]


def owner_kernel(arrived_ref, fields_ref, reply_ref):
    group = lax.broadcasted_iota(jnp.int32, (32, 128), 1) // CAP
    cells = jnp.zeros((32, 128), jnp.int32)
    for member in range(4):
        cells = jnp.where(group == member, arrived_ref[member * 32 : member * 32 + 32, :], cells)
    block = cells >> 7
    key = ((cells >> 6) & 1) * 128 + ((block >> 5) * 4 + (block & 3)) * 8 + ((block >> 2) & 7)
    spot = cells & 63

    tables = []
    for c in range(4):
        rows = jnp.concatenate(
            [fields_ref[c, x, :, z * 128 : (z + 1) * 128] for x in range(4) for z in range(4)],
            axis=0,
        )
        rows = jnp.transpose(rows)
        rows = jnp.concatenate([rows[:64], rows[64:]], axis=1)
        tables.append(jnp.concatenate(thirds(rows), axis=1).astype(BF16))
    table = jnp.concatenate(tables, axis=0)

    row = lax.broadcasted_iota(jnp.int32, (256, 128), 0).astype(F32).astype(BF16)
    key = key.astype(F32)
    one, none = jnp.ones((), BF16), jnp.zeros((), BF16)
    lane = lax.broadcasted_iota(jnp.int32, (64, 128), 0)
    for g in range(0, 32, 8):
        hot = jnp.concatenate(
            [jnp.where(row == key[g + j : g + j + 1].astype(BF16), one, none) for j in range(8)],
            axis=1,
        )
        looked = dot(table, jnp.concatenate([hot, hot, hot], axis=0), NN)
        for j in range(8):
            mine = lane == spot[g + j : g + j + 1]
            found = jnp.concatenate(
                [
                    jnp.sum(
                        jnp.where(mine, looked[c * 64 : c * 64 + 64, j * 128 : j * 128 + 128], 0.0),
                        axis=0,
                        keepdims=True,
                    )
                    for c in range(4)
                ],
                axis=0,
            )
            for member in range(4):
                turned = found if member == 0 else pltpu.roll(found, 128 - CAP * member, 1)
                reply_ref[member * 32 + g + j] = turned


def thirds(x):
    high = x.astype(BF16).astype(F32)
    rest = x - high
    middle = rest.astype(BF16).astype(F32)
    low = (rest - middle).astype(BF16).astype(F32)
    return high, middle, low


def emit_kernel(scale, returned_ref, *refs):
    *shared_refs, at_ref, observer_ref, signal_ref = refs
    members = len(shared_refs)
    panels = shared_refs[0].shape[1]

    def unfold(ref, row):
        return jnp.concatenate([ref[row, j : j + 1, :] for j in range(8)], axis=1)

    at = at_ref[0]
    observers = observer_ref[:, pl.ds(pl.multiple_of(at * 512, 512), 512)]
    ox, oy, oz = observers[0:1], observers[1:2], observers[2:3]
    none = jnp.zeros_like(ox)
    features = jnp.concatenate(
        [ox, oy, oz, none + 1.0, ox * ox + oy * oy + oz * oz, none, none, none], axis=0
    )
    h, m, w = thirds(features)
    seen = jnp.transpose(jnp.concatenate([h, m, h, m, w, h], axis=0)).astype(BF16)

    table = thirds(
        jnp.concatenate([jnp.transpose(returned_ref[:, c, :]) for c in range(4)], axis=0)
    )[:2]
    device = lax.broadcasted_iota(jnp.int32, (128, panels), 0).astype(F32).astype(BF16)
    place = lax.broadcasted_iota(jnp.int32, (CAP, panels), 0).astype(F32)
    level = lax.broadcasted_iota(jnp.int32, (BINS, panels), 0).astype(F32).astype(BF16)
    zero = jnp.zeros((1, panels), F32)
    one, none = jnp.ones((), BF16), jnp.zeros((), BF16)
    total = [None] * 4
    for member in range(members):
        shared_ref = shared_refs[member]
        if member == 0:
            bins = shared_ref[0:4, :]
            for k in range(1, 4):
                bins = jnp.where(at == k, shared_ref[4 * k : 4 * k + 4, :], bins)
            px, py, pz, area, owner, rank = (shared_ref[16 + j : 17 + j, :] for j in range(6))
        else:
            bins = jnp.concatenate([unfold(shared_ref, b) for b in range(4)], axis=0)
            px, py, pz, area, owner, rank = (unfold(shared_ref, 4 + j) for j in range(6))
        mine = [
            jnp.concatenate(
                [part[c * 128 + member * CAP :][:CAP] for c in range(4)],
                axis=0,
            )
            for part in table
        ]
        rows = jnp.concatenate(mine, axis=1).astype(BF16)
        hot = jnp.where(device == owner.astype(BF16), one, none)
        looked = dot(rows, jnp.concatenate([hot, hot], axis=0), NN)
        here = place == rank
        area = area * scale
        s = [
            area
            * jnp.sum(jnp.where(here, looked[c * CAP : (c + 1) * CAP], 0.0), axis=0, keepdims=True)
            for c in range(4)
        ]
        along = jnp.concatenate(
            [s[1], s[2], s[3], -(s[1] * px + s[2] * py + s[3] * pz), zero, zero, zero, zero], axis=0
        )
        square = jnp.concatenate(
            [-2.0 * px, -2.0 * py, -2.0 * pz, px * px + py * py + pz * pz, zero + 1.0, zero, zero, zero],
            axis=0,
        )
        h, m, w = thirds(along)
        along = jnp.concatenate([h, h, m, m, h, w], axis=0).astype(BF16)
        h, m, w = thirds(square)
        square = jnp.concatenate([h, h, m, m, h, w], axis=0).astype(BF16)
        inverse = lax.rsqrt(dot(seen, square, NN))
        along = dot(seen, along, NN)
        emitted = ((along * inverse + s[0]) * inverse).astype(BF16)
        bins = bins.astype(BF16)
        for b in range(4):
            span = slice(b * OB, (b + 1) * OB)
            hot = jnp.where(bins[b : b + 1] == level, one, none)
            term = dot(emitted[span], hot, NT)
            total[b] = term if member == 0 else total[b] + term
    for b in range(4):
        signal_ref[b * OB : (b + 1) * OB, :] = total[b]


def rim_kernel(odd_ref, fields_ref, velocity_ref, left_ref, right_ref, near_ref, far_ref):
    odd = odd_ref[0] == 1

    def put(spot, low, high):
        near_ref[spot] = jnp.where(odd, low, high)
        far_ref[spot] = jnp.where(odd, high, low)

    for c in range(4):
        for x in range(4):
            column = fields_ref[c, x]
            put(4 * c + x, column[0:4], column[4:8])
        for side in range(2):
            one, two = (
                column_of(fields_ref, left_ref, right_ref, c, x)
                for x in ((-2, -1) if side == 0 else (4, 5))
            )
            put(
                22 + 2 * c + side,
                jnp.concatenate([one[0:2], two[0:2]], axis=0),
                jnp.concatenate([one[6:8], two[6:8]], axis=0),
            )
    for k in range(3):
        for half in range(2):
            one, two = velocity_ref[k, 2 * half], velocity_ref[k, 2 * half + 1]
            put(
                16 + 2 * k + half,
                jnp.concatenate([one[0:2], two[0:2]], axis=0),
                jnp.concatenate([one[6:8], two[6:8]], axis=0),
            )


def column_of(fields_ref, left_ref, right_ref, c, x):
    if x < 0:
        return left_ref[4 * c + x + 4]
    if x >= 4:
        return right_ref[4 * c + x - 4]
    return fields_ref[c, x]


def rate(center, across, tall, velocity, diffusion):
    rows, width = center.shape
    near = [
        (across[2], across[1]),
        (tall[3 : 3 + rows], tall[1 : 1 + rows]),
        (pltpu.roll(center, width - 1, 1), pltpu.roll(center, 1, 1)),
    ]
    far = [
        (across[3], across[0]),
        (tall[4 : 4 + rows], tall[0:rows]),
        (pltpu.roll(center, width - 2, 1), pltpu.roll(center, 2, 1)),
    ]
    advect = 0.0
    spread = -90.0 * center
    for k in range(3):
        advect = advect + velocity[k] * (
            8.0 * (near[k][0] - near[k][1]) - (far[k][0] - far[k][1])
        )
        spread = spread + (16.0 * (near[k][0] + near[k][1]) - (far[k][0] + far[k][1]))
    return (diffusion * spread - advect) * (1.0 / 12.0)


def transport_kernel(
    diffusion_ref, odd_ref, fields_ref, velocity_ref, left_ref, right_ref, near_ref, far_ref, out_ref
):
    odd = odd_ref[0] == 1

    def low(spot):
        return jnp.where(odd, near_ref[spot], far_ref[spot])

    def high(spot):
        return jnp.where(odd, far_ref[spot], near_ref[spot])

    for c in range(4):
        diffusion = diffusion_ref[c]

        def column(x):
            return column_of(fields_ref, left_ref, right_ref, c, x)

        below = {x: low(4 * c + x) for x in range(4)}
        above = {x: high(4 * c + x) for x in range(4)}
        tall = {
            x: jnp.concatenate([below[x][2:4], column(x), above[x][0:2]], axis=0) for x in range(4)
        }
        for side in range(2):
            under, over = low(22 + 2 * c + side), high(22 + 2 * c + side)
            for i in range(2):
                x, part = (-2 + i, 4 + i)[side], slice(2 * i, 2 * i + 2)
                tall[x] = jnp.concatenate([under[part], column(x), over[part]], axis=0)
        middle = {}
        taller = {}
        for x in range(4):
            center = tall[x]
            wide = jnp.concatenate([below[x][0:2], center, above[x][2:4]], axis=0)
            velocity = []
            for k in range(3):
                spot, part = 16 + 2 * k + x // 2, slice(2 * (x % 2), 2 * (x % 2) + 2)
                velocity.append(
                    jnp.concatenate(
                        [low(spot)[part], velocity_ref[k, x], high(spot)[part]], axis=0
                    )
                )
            across = [tall[x + d] for d in (-2, -1, 1, 2)]
            taller[x] = center + TIME_STEP * rate(center, across, wide, velocity, diffusion)
            middle[x] = taller[x][2:10]
        for x in (-2, -1, 4, 5):
            center = column(x)
            side, spot = (left_ref, x + 2) if x < 0 else (right_ref, x - 4)
            velocity = [side[16 + 2 * k + spot] for k in range(3)]
            across = [column(x + d) for d in (-2, -1, 1, 2)]
            middle[x] = center + TIME_STEP * rate(center, across, tall[x], velocity, diffusion)
        for x in range(4):
            velocity = [velocity_ref[k, x] for k in range(3)]
            across = [middle[x + d] for d in (-2, -1, 1, 2)]
            change = rate(middle[x], across, taller[x], velocity, diffusion)
            out_ref[c, x] = 0.5 * fields_ref[c, x] + 0.5 * (middle[x] + TIME_STEP * change)


def neighbours(axis, count, head, tail):
    return (
        lax.ppermute(tail, axis, [(i, (i + 1) % count) for i in range(count)]),
        lax.ppermute(head, axis, [((i + 1) % count, i) for i in range(count)]),
    )


def exchange(array, axes):
    return lax.all_to_all(array, axes, split_axis=0, concat_axis=0, tiled=True)


VM = pl.BlockSpec(memory_space=pltpu.VMEM)
ANY = pl.BlockSpec(memory_space=pl.ANY)
SM = pl.BlockSpec(memory_space=pltpu.SMEM)


def call(kernel, outs, in_specs, args, name, flops, moved, limit=VMEM_LIMIT):
    return pl.pallas_call(
        kernel,
        out_shape=outs,
        in_specs=in_specs,
        out_specs=jax.tree.map(lambda _: VM, outs),
        compiler_params=pltpu.CompilerParams(vmem_limit_bytes=limit),
        cost_estimate=pl.CostEstimate(flops=flops, bytes_accessed=moved, transcendentals=0),
        name=name,
    )(*args)


def ask(owner, cell, bins, position, area, fields, velocity):
    panels = owner.shape[1]
    side = jax.ShapeDtypeStruct((22, 8, 512), F32)
    return pl.pallas_call(
        ask_kernel,
        out_shape=(
            jax.ShapeDtypeStruct((128, 128), jnp.int32),
            jax.ShapeDtypeStruct((24, panels), F32),
            side,
            side,
        ),
        in_specs=[ANY] * 7,
        out_specs=(VM, VM, VM, VM),
        scratch_shapes=[
            pltpu.VMEM((1, panels), jnp.int32),
            pltpu.VMEM((1, panels), jnp.int32),
            pltpu.VMEM((16, panels), jnp.int32),
            pltpu.VMEM((3, panels), F32),
            pltpu.VMEM((1, panels), F32),
            pltpu.SemaphoreType.DMA((19,)),
        ],
        cost_estimate=pl.CostEstimate(flops=2_000_000, bytes_accessed=100_000, transcendentals=0),
        compiler_params=pltpu.CompilerParams(vmem_limit_bytes=FULL_VMEM),
        name="ask",
    )(owner, cell, bins, position, area, fields, velocity)


def per_device(
    fields,
    velocity,
    diffusion,
    panel_owner,
    panel_cell,
    panel_bins,
    panel_position,
    panel_area,
    observer_position,
):
    shape = jax.ShapeDtypeStruct
    after = lax.optimization_barrier
    panels = panel_cell.shape[0]
    every = ("hi", "lo", "gy")
    rims = shape((30, 4, 512), F32)

    requests, share, head, tail = ask(
        panel_owner.reshape(1, panels),
        panel_cell.reshape(1, panels),
        panel_bins,
        panel_position,
        panel_area.reshape(1, panels),
        fields,
        velocity,
    )
    arrived = exchange(requests, every)

    left, right = neighbours(("hi", "lo"), 32, head, tail)
    at = lax.axis_index("hi").reshape(1)
    few = shape((10, 8, 128), F32)
    packed = call(
        pack_kernel,
        (few, few, few),
        [SM, VM],
        (at, share),
        "pack",
        100_000,
        250_000,
    )
    arrived = after((arrived, *packed))[0]
    group = [share]
    for k in range(1, 4):
        group.append(lax.ppermute(packed[k - 1], "hi", [(i, (i - k) % 4) for i in range(4)]))

    reply = call(
        owner_kernel,
        shape((128, 4, 128), F32),
        [VM] * 2,
        (arrived, fields),
        "sample",
        5_000_000_000,
        600_000,
    )
    returned = exchange(reply, every)

    left, right, _ = after((left, right, reply))
    odd = (lax.axis_index("gy") % 2).reshape(1)
    near, far = call(
        rim_kernel,
        (rims, rims),
        [SM] + [VM] * 4,
        (odd, fields, velocity, left, right),
        "rim",
        100_000,
        2_000_000,
    )
    returned = after((returned, near, far))[0]
    near = lax.ppermute(near, "gy", [(0, 1), (1, 0), (2, 3), (3, 2)])
    far = lax.ppermute(far, "gy", [(1, 2), (2, 1), (3, 0), (0, 3)])

    scale = (BINS / (panels * 128)) ** 0.5
    partial = call(
        functools.partial(emit_kernel, scale),
        shape((512, BINS), F32),
        [VM] * 5 + [SM, VM],
        (returned, *group, at, observer_position),
        "emit",
        5_000_000_000,
        800_000,
    )
    parts = exchange(partial.reshape(32, 16, BINS), ("lo", "gy"))

    near, far, _ = after((near, far, partial))
    advanced = call(
        transport_kernel,
        shape(fields.shape, F32),
        [SM, SM] + [VM] * 6,
        (diffusion, odd, fields, velocity, left, right, near, far),
        "transport",
        5_000_000_000,
        3_000_000,
    )
    parts, advanced = after((parts, advanced))
    return advanced, jnp.sum(parts, axis=0)


def solution(mesh):
    count_x, count_y = mesh.devices.shape
    split = Mesh(mesh.devices.reshape(4, count_x // 4, count_y), ("hi", "lo", "gy"))
    gx = ("hi", "lo")
    every = ("hi", "lo", "gy")

    in_specs = (
        P(None, gx, "gy", None),
        P(None, gx, "gy", None),
        P(),
        P(every, None),
        P(every),
        P(None, every),
        P(None, every),
        P(every),
        P(),
    )
    out_specs = (P(None, gx, "gy", None), P(every, None))
    return jax.shard_map(
        per_device, mesh=split, in_specs=in_specs, out_specs=out_specs, check_vma=False
    )
```

```python
import functools

import jax
import jax.numpy as jnp
from jax import lax
from jax.experimental import pallas as pl
from jax.experimental.pallas import tpu as pltpu
from jax.sharding import Mesh
from jax.sharding import PartitionSpec as P

OBS = 2048
BINS = 128
OB = 128
CAP = 32
TIME_STEP = 0.15
VMEM_LIMIT = 48 * 1024 * 1024
FULL_VMEM = 60 * 1024 * 1024
F32 = jnp.float32
BF16 = jnp.bfloat16
NT = (((1,), (1,)), ((), ()))
NN = (((1,), (0,)), ((), ()))


def dot(a, b, dims):
    return lax.dot_general(a, b, dims, preferred_element_type=F32)


def ask_kernel(
    owner_in,
    cell_in,
    bins_in,
    position_in,
    area_in,
    fields_in,
    velocity_in,
    request_ref,
    share_ref,
    head_ref,
    tail_ref,
    owner_ref,
    cell_ref,
    bins_ref,
    position_ref,
    area_ref,
    arrival,
):
    pairs = [
        (owner_in, owner_ref),
        (cell_in, cell_ref),
        (bins_in, bins_ref),
        (position_in, position_ref),
        (area_in, area_ref),
    ]
    for out, first in ((head_ref, 0), (tail_ref, 2)):
        for c in range(4):
            pairs.append((fields_in.at[c], out.at[pl.ds(4 * c, 4)]))
        for k in range(3):
            pairs.append((velocity_in.at[k, pl.ds(first, 2)], out.at[pl.ds(16 + 2 * k, 2)]))
    loads = [
        pltpu.make_async_copy(source, target, arrival.at[i])
        for i, (source, target) in enumerate(pairs)
    ]
    for load in loads:
        load.start()
    panels = owner_ref.shape[1]
    chunk = 256
    ahead = lax.broadcasted_iota(jnp.int32, (chunk, 2 * chunk), 0)
    behind = lax.broadcasted_iota(jnp.int32, (chunk, 2 * chunk), 1)
    before = jnp.where((ahead < behind) | (behind >= chunk), 1.0, 0.0).astype(BF16)
    device = lax.broadcasted_iota(jnp.int32, (128, chunk), 0)
    place = lax.broadcasted_iota(jnp.int32, (CAP, chunk), 0).astype(F32)
    running = jnp.zeros((128, chunk), F32)
    table = jnp.zeros((128, 2 * CAP), F32)
    for load in loads[:2]:
        load.wait()
    for k in range(panels // chunk):
        span = slice(k * chunk, (k + 1) * chunk)
        owner = owner_ref[:, span]
        cell = cell_ref[:, span]
        hit = jnp.where(device == owner, 1.0, 0.0)
        hot = hit.astype(BF16)
        counted = dot(hot, before, NN)
        rank = jnp.sum(hit * (counted[:, :chunk] + running), axis=0, keepdims=True)
        running = running + counted[:, chunk:]
        mine = place == rank
        high = jnp.where(mine, (cell >> 7).astype(F32), 0.0)
        low = jnp.where(mine, (cell & 127).astype(F32), 0.0)
        table = table + dot(hot, jnp.concatenate([high, low], axis=0).astype(BF16), NT)
        share_ref[20:21, span] = owner.astype(F32)
        share_ref[21:22, span] = rank
    asked = (table[:, :CAP] * 128.0 + table[:, CAP:]).astype(jnp.int32)
    request_ref[...] = jnp.concatenate([asked, asked, asked, asked], axis=1)
    for load in loads[2:]:
        load.wait()
    share_ref[0:16, :] = bins_ref[...].astype(F32)
    share_ref[16:19, :] = position_ref[...]
    share_ref[19:20, :] = area_ref[...]
    share_ref[22:24, :] = jnp.zeros((2, panels), F32)


def pack_kernel(at_ref, share_ref, *outs):
    def fold(row):
        line = share_ref[row : row + 1, :]
        return jnp.concatenate([line[:, j * 128 : j * 128 + 128] for j in range(8)], axis=0)

    folded = [fold(row) for row in range(22)]
    for k in range(1, 4):
        to = (at_ref[0] + (4 - k)) % 4
        for b in range(4):
            rows = folded[b]
            for member in range(1, 4):
                rows = jnp.where(to == member, folded[4 * member + b], rows)
            outs[k - 1][b] = rows
        for j in range(6):
            outs[k - 1][4 + j] = folded[16 + j]


def owner_kernel(arrived_ref, fields_ref, reply_ref):
    group = lax.broadcasted_iota(jnp.int32, (32, 128), 1) // CAP
    cells = jnp.zeros((32, 128), jnp.int32)
    for member in range(4):
        cells = jnp.where(group == member, arrived_ref[member * 32 : member * 32 + 32, :], cells)
    block = cells >> 7
    key = ((cells >> 6) & 1) * 128 + ((block >> 5) * 4 + (block & 3)) * 8 + ((block >> 2) & 7)
    spot = cells & 63

    tables = []
    for c in range(4):
        rows = jnp.concatenate(
            [fields_ref[c, x, :, z * 128 : (z + 1) * 128] for x in range(4) for z in range(4)],
            axis=0,
        )
        rows = jnp.transpose(rows)
        rows = jnp.concatenate([rows[:64], rows[64:]], axis=1)
        tables.append(jnp.concatenate(thirds(rows), axis=1).astype(BF16))
    table = jnp.concatenate(tables, axis=0)

    row = lax.broadcasted_iota(jnp.int32, (256, 128), 0).astype(F32).astype(BF16)
    key = key.astype(F32)
    one, none = jnp.ones((), BF16), jnp.zeros((), BF16)
    lane = lax.broadcasted_iota(jnp.int32, (64, 128), 0)
    for g in range(0, 32, 8):
        hot = jnp.concatenate(
            [jnp.where(row == key[g + j : g + j + 1].astype(BF16), one, none) for j in range(8)],
            axis=1,
        )
        looked = dot(table, jnp.concatenate([hot, hot, hot], axis=0), NN)
        for j in range(8):
            mine = lane == spot[g + j : g + j + 1]
            found = jnp.concatenate(
                [
                    jnp.sum(
                        jnp.where(mine, looked[c * 64 : c * 64 + 64, j * 128 : j * 128 + 128], 0.0),
                        axis=0,
                        keepdims=True,
                    )
                    for c in range(4)
                ],
                axis=0,
            )
            for member in range(4):
                turned = found if member == 0 else pltpu.roll(found, 128 - CAP * member, 1)
                reply_ref[member * 32 + g + j] = turned


def thirds(x):
    high = x.astype(BF16).astype(F32)
    rest = x - high
    middle = rest.astype(BF16).astype(F32)
    low = (rest - middle).astype(BF16).astype(F32)
    return high, middle, low


def emit_kernel(scale, returned_ref, *refs):
    *shared_refs, at_ref, observer_ref, signal_ref = refs
    members = len(shared_refs)
    panels = shared_refs[0].shape[1]

    def unfold(ref, row):
        return jnp.concatenate([ref[row, j : j + 1, :] for j in range(8)], axis=1)

    at = at_ref[0]
    observers = observer_ref[:, pl.ds(pl.multiple_of(at * 512, 512), 512)]
    ox, oy, oz = observers[0:1], observers[1:2], observers[2:3]
    none = jnp.zeros_like(ox)
    features = jnp.concatenate(
        [ox, oy, oz, none + 1.0, ox * ox + oy * oy + oz * oz, none, none, none], axis=0
    )
    h, m, w = thirds(features)
    seen = jnp.transpose(jnp.concatenate([h, m, h, m, w, h], axis=0)).astype(BF16)

    table = thirds(
        jnp.concatenate([jnp.transpose(returned_ref[:, c, :]) for c in range(4)], axis=0)
    )[:2]
    device = lax.broadcasted_iota(jnp.int32, (128, panels), 0).astype(F32).astype(BF16)
    place = lax.broadcasted_iota(jnp.int32, (CAP, panels), 0).astype(F32)
    level = lax.broadcasted_iota(jnp.int32, (BINS, panels), 0).astype(F32).astype(BF16)
    zero = jnp.zeros((1, panels), F32)
    one, none = jnp.ones((), BF16), jnp.zeros((), BF16)
    total = [None] * 4
    for member in range(members):
        shared_ref = shared_refs[member]
        if member == 0:
            bins = shared_ref[0:4, :]
            for k in range(1, 4):
                bins = jnp.where(at == k, shared_ref[4 * k : 4 * k + 4, :], bins)
            px, py, pz, area, owner, rank = (shared_ref[16 + j : 17 + j, :] for j in range(6))
        else:
            bins = jnp.concatenate([unfold(shared_ref, b) for b in range(4)], axis=0)
            px, py, pz, area, owner, rank = (unfold(shared_ref, 4 + j) for j in range(6))
        mine = [
            jnp.concatenate(
                [part[c * 128 + member * CAP :][:CAP] for c in range(4)],
                axis=0,
            )
            for part in table
        ]
        rows = jnp.concatenate(mine, axis=1).astype(BF16)
        hot = jnp.where(device == owner.astype(BF16), one, none)
        looked = dot(rows, jnp.concatenate([hot, hot], axis=0), NN)
        here = place == rank
        area = area * scale
        s = [
            area
            * jnp.sum(jnp.where(here, looked[c * CAP : (c + 1) * CAP], 0.0), axis=0, keepdims=True)
            for c in range(4)
        ]
        along = jnp.concatenate(
            [s[1], s[2], s[3], -(s[1] * px + s[2] * py + s[3] * pz), zero, zero, zero, zero], axis=0
        )
        square = jnp.concatenate(
            [-2.0 * px, -2.0 * py, -2.0 * pz, px * px + py * py + pz * pz, zero + 1.0, zero, zero, zero],
            axis=0,
        )
        h, m, w = thirds(along)
        along = jnp.concatenate([h, h, m, m, h, w], axis=0).astype(BF16)
        h, m, w = thirds(square)
        square = jnp.concatenate([h, h, m, m, h, w], axis=0).astype(BF16)
        inverse = lax.rsqrt(dot(seen, square, NN))
        along = dot(seen, along, NN)
        emitted = ((along * inverse + s[0]) * inverse).astype(BF16)
        bins = bins.astype(BF16)
        for b in range(4):
            span = slice(b * OB, (b + 1) * OB)
            hot = jnp.where(bins[b : b + 1] == level, one, none)
            term = dot(emitted[span], hot, NT)
            total[b] = term if member == 0 else total[b] + term
    for b in range(4):
        signal_ref[b * OB : (b + 1) * OB, :] = total[b]


def rim_kernel(odd_ref, fields_ref, velocity_ref, left_ref, right_ref, near_ref, far_ref):
    odd = odd_ref[0] == 1

    def put(spot, low, high):
        near_ref[spot] = jnp.where(odd, low, high)
        far_ref[spot] = jnp.where(odd, high, low)

    for c in range(4):
        for x in range(4):
            column = fields_ref[c, x]
            put(4 * c + x, column[0:4], column[4:8])
        for side in range(2):
            one, two = (
                column_of(fields_ref, left_ref, right_ref, c, x)
                for x in ((-2, -1) if side == 0 else (4, 5))
            )
            put(
                22 + 2 * c + side,
                jnp.concatenate([one[0:2], two[0:2]], axis=0),
                jnp.concatenate([one[6:8], two[6:8]], axis=0),
            )
    for k in range(3):
        for half in range(2):
            one, two = velocity_ref[k, 2 * half], velocity_ref[k, 2 * half + 1]
            put(
                16 + 2 * k + half,
                jnp.concatenate([one[0:2], two[0:2]], axis=0),
                jnp.concatenate([one[6:8], two[6:8]], axis=0),
            )


def column_of(fields_ref, left_ref, right_ref, c, x):
    if x < 0:
        return left_ref[4 * c + x + 4]
    if x >= 4:
        return right_ref[4 * c + x - 4]
    return fields_ref[c, x]


def rate(center, across, tall, velocity, diffusion):
    rows, width = center.shape
    near = [
        (across[2], across[1]),
        (tall[3 : 3 + rows], tall[1 : 1 + rows]),
        (pltpu.roll(center, width - 1, 1), pltpu.roll(center, 1, 1)),
    ]
    far = [
        (across[3], across[0]),
        (tall[4 : 4 + rows], tall[0:rows]),
        (pltpu.roll(center, width - 2, 1), pltpu.roll(center, 2, 1)),
    ]
    advect = 0.0
    spread = -90.0 * center
    for k in range(3):
        advect = advect + velocity[k] * (
            8.0 * (near[k][0] - near[k][1]) - (far[k][0] - far[k][1])
        )
        spread = spread + (16.0 * (near[k][0] + near[k][1]) - (far[k][0] + far[k][1]))
    return (diffusion * spread - advect) * (1.0 / 12.0)


def transport_kernel(
    diffusion_ref, odd_ref, fields_ref, velocity_ref, left_ref, right_ref, near_ref, far_ref, out_ref
):
    odd = odd_ref[0] == 1

    def low(spot):
        return jnp.where(odd, near_ref[spot], far_ref[spot])

    def high(spot):
        return jnp.where(odd, far_ref[spot], near_ref[spot])

    for c in range(4):
        diffusion = diffusion_ref[c]

        def column(x):
            return column_of(fields_ref, left_ref, right_ref, c, x)

        below = {x: low(4 * c + x) for x in range(4)}
        above = {x: high(4 * c + x) for x in range(4)}
        tall = {
            x: jnp.concatenate([below[x][2:4], column(x), above[x][0:2]], axis=0) for x in range(4)
        }
        for side in range(2):
            under, over = low(22 + 2 * c + side), high(22 + 2 * c + side)
            for i in range(2):
                x, part = (-2 + i, 4 + i)[side], slice(2 * i, 2 * i + 2)
                tall[x] = jnp.concatenate([under[part], column(x), over[part]], axis=0)
        middle = {}
        taller = {}
        for x in range(4):
            center = tall[x]
            wide = jnp.concatenate([below[x][0:2], center, above[x][2:4]], axis=0)
            velocity = []
            for k in range(3):
                spot, part = 16 + 2 * k + x // 2, slice(2 * (x % 2), 2 * (x % 2) + 2)
                velocity.append(
                    jnp.concatenate(
                        [low(spot)[part], velocity_ref[k, x], high(spot)[part]], axis=0
                    )
                )
            across = [tall[x + d] for d in (-2, -1, 1, 2)]
            taller[x] = center + TIME_STEP * rate(center, across, wide, velocity, diffusion)
            middle[x] = taller[x][2:10]
        for x in (-2, -1, 4, 5):
            center = column(x)
            side, spot = (left_ref, x + 2) if x < 0 else (right_ref, x - 4)
            velocity = [side[16 + 2 * k + spot] for k in range(3)]
            across = [column(x + d) for d in (-2, -1, 1, 2)]
            middle[x] = center + TIME_STEP * rate(center, across, tall[x], velocity, diffusion)
        for x in range(4):
            velocity = [velocity_ref[k, x] for k in range(3)]
            across = [middle[x + d] for d in (-2, -1, 1, 2)]
            change = rate(middle[x], across, taller[x], velocity, diffusion)
            out_ref[c, x] = 0.5 * fields_ref[c, x] + 0.5 * (middle[x] + TIME_STEP * change)


def neighbours(axis, count, head, tail):
    return (
        lax.ppermute(tail, axis, [(i, (i + 1) % count) for i in range(count)]),
        lax.ppermute(head, axis, [((i + 1) % count, i) for i in range(count)]),
    )


def exchange(array, axes):
    return lax.all_to_all(array, axes, split_axis=0, concat_axis=0, tiled=True)


VM = pl.BlockSpec(memory_space=pltpu.VMEM)
ANY = pl.BlockSpec(memory_space=pl.ANY)
SM = pl.BlockSpec(memory_space=pltpu.SMEM)


def call(kernel, outs, in_specs, args, name, flops, moved, limit=VMEM_LIMIT):
    return pl.pallas_call(
        kernel,
        out_shape=outs,
        in_specs=in_specs,
        out_specs=jax.tree.map(lambda _: VM, outs),
        compiler_params=pltpu.CompilerParams(vmem_limit_bytes=limit),
        cost_estimate=pl.CostEstimate(flops=flops, bytes_accessed=moved, transcendentals=0),
        name=name,
    )(*args)


def ask(owner, cell, bins, position, area, fields, velocity):
    panels = owner.shape[1]
    side = jax.ShapeDtypeStruct((22, 8, 512), F32)
    return pl.pallas_call(
        ask_kernel,
        out_shape=(
            jax.ShapeDtypeStruct((128, 128), jnp.int32),
            jax.ShapeDtypeStruct((24, panels), F32),
            side,
            side,
        ),
        in_specs=[ANY] * 7,
        out_specs=(VM, VM, VM, VM),
        scratch_shapes=[
            pltpu.VMEM((1, panels), jnp.int32),
            pltpu.VMEM((1, panels), jnp.int32),
            pltpu.VMEM((16, panels), jnp.int32),
            pltpu.VMEM((3, panels), F32),
            pltpu.VMEM((1, panels), F32),
            pltpu.SemaphoreType.DMA((19,)),
        ],
        cost_estimate=pl.CostEstimate(flops=2_000_000, bytes_accessed=100_000, transcendentals=0),
        compiler_params=pltpu.CompilerParams(vmem_limit_bytes=FULL_VMEM),
        name="ask",
    )(owner, cell, bins, position, area, fields, velocity)


def per_device(
    fields,
    velocity,
    diffusion,
    panel_owner,
    panel_cell,
    panel_bins,
    panel_position,
    panel_area,
    observer_position,
):
    shape = jax.ShapeDtypeStruct
    after = lax.optimization_barrier
    panels = panel_cell.shape[0]
    every = ("hi", "lo", "gy")
    rims = shape((30, 4, 512), F32)

    requests, share, head, tail = ask(
        panel_owner.reshape(1, panels),
        panel_cell.reshape(1, panels),
        panel_bins,
        panel_position,
        panel_area.reshape(1, panels),
        fields,
        velocity,
    )
    arrived = exchange(requests, every)

    left, right = neighbours(("hi", "lo"), 32, head, tail)
    at = lax.axis_index("hi").reshape(1)
    few = shape((10, 8, 128), F32)
    packed = call(
        pack_kernel,
        (few, few, few),
        [SM, VM],
        (at, share),
        "pack",
        100_000,
        250_000,
    )
    arrived = after((arrived, *packed))[0]
    group = [share]
    for k in range(1, 4):
        group.append(lax.ppermute(packed[k - 1], "hi", [(i, (i - k) % 4) for i in range(4)]))

    reply = call(
        owner_kernel,
        shape((128, 4, 128), F32),
        [VM] * 2,
        (arrived, fields),
        "sample",
        5_000_000_000,
        600_000,
    )
    reply, group[2] = after((reply, group[2]))
    returned = exchange(reply, every)

    left, right, _ = after((left, right, reply))
    odd = (lax.axis_index("gy") % 2).reshape(1)
    near, far = call(
        rim_kernel,
        (rims, rims),
        [SM] + [VM] * 4,
        (odd, fields, velocity, left, right),
        "rim",
        100_000,
        2_000_000,
    )
    returned = after((returned, near, far))[0]
    near = lax.ppermute(near, "gy", [(0, 1), (1, 0), (2, 3), (3, 2)])
    far = lax.ppermute(far, "gy", [(1, 2), (2, 1), (3, 0), (0, 3)])

    scale = (BINS / (panels * 128)) ** 0.5
    partial = call(
        functools.partial(emit_kernel, scale),
        shape((512, BINS), F32),
        [VM] * 5 + [SM, VM],
        (returned, *group, at, observer_position),
        "emit",
        5_000_000_000,
        800_000,
    )
    parts = exchange(partial.reshape(32, 16, BINS), ("lo", "gy"))

    near, far, _ = after((near, far, partial))
    advanced = call(
        transport_kernel,
        shape(fields.shape, F32),
        [SM, SM] + [VM] * 6,
        (diffusion, odd, fields, velocity, left, right, near, far),
        "transport",
        5_000_000_000,
        3_000_000,
    )
    parts, advanced = after((parts, advanced))
    return advanced, jnp.sum(parts, axis=0)


def solution(mesh):
    count_x, count_y = mesh.devices.shape
    split = Mesh(mesh.devices.reshape(4, count_x // 4, count_y), ("hi", "lo", "gy"))
    gx = ("hi", "lo")
    every = ("hi", "lo", "gy")

    in_specs = (
        P(None, gx, "gy", None),
        P(None, gx, "gy", None),
        P(),
        P(every, None),
        P(every),
        P(None, every),
        P(None, every),
        P(every),
        P(),
    )
    out_specs = (P(None, gx, "gy", None), P(every, None))
    return jax.shard_map(
        per_device, mesh=split, in_specs=in_specs, out_specs=out_specs, check_vma=False
    )
```

```python
import functools

import jax
import jax.numpy as jnp
from jax import lax
from jax.experimental import pallas as pl
from jax.experimental.pallas import tpu as pltpu
from jax.sharding import Mesh
from jax.sharding import PartitionSpec as P

OBS = 2048
BINS = 128
OB = 128
CAP = 32
TIME_STEP = 0.15
VMEM_LIMIT = 48 * 1024 * 1024
FULL_VMEM = 60 * 1024 * 1024
F32 = jnp.float32
BF16 = jnp.bfloat16
NT = (((1,), (1,)), ((), ()))
NN = (((1,), (0,)), ((), ()))


def dot(a, b, dims):
    return lax.dot_general(a, b, dims, preferred_element_type=F32)


def ask_kernel(
    owner_in,
    cell_in,
    bins_in,
    position_in,
    area_in,
    fields_in,
    velocity_in,
    request_ref,
    share_ref,
    head_ref,
    tail_ref,
    owner_ref,
    cell_ref,
    bins_ref,
    position_ref,
    area_ref,
    arrival,
):
    pairs = [
        (owner_in, owner_ref),
        (cell_in, cell_ref),
        (bins_in, bins_ref),
        (position_in, position_ref),
        (area_in, area_ref),
    ]
    for out, first in ((head_ref, 0), (tail_ref, 2)):
        for c in range(4):
            pairs.append((fields_in.at[c], out.at[pl.ds(4 * c, 4)]))
        for k in range(3):
            pairs.append((velocity_in.at[k, pl.ds(first, 2)], out.at[pl.ds(16 + 2 * k, 2)]))
    loads = [
        pltpu.make_async_copy(source, target, arrival.at[i])
        for i, (source, target) in enumerate(pairs)
    ]
    for load in loads:
        load.start()
    panels = owner_ref.shape[1]
    chunk = 256
    ahead = lax.broadcasted_iota(jnp.int32, (chunk, 2 * chunk), 0)
    behind = lax.broadcasted_iota(jnp.int32, (chunk, 2 * chunk), 1)
    before = jnp.where((ahead < behind) | (behind >= chunk), 1.0, 0.0).astype(BF16)
    device = lax.broadcasted_iota(jnp.int32, (128, chunk), 0)
    place = lax.broadcasted_iota(jnp.int32, (CAP, chunk), 0).astype(F32)
    running = jnp.zeros((128, chunk), F32)
    table = jnp.zeros((128, 2 * CAP), F32)
    for load in loads[:2]:
        load.wait()
    for k in range(panels // chunk):
        span = slice(k * chunk, (k + 1) * chunk)
        owner = owner_ref[:, span]
        cell = cell_ref[:, span]
        hit = jnp.where(device == owner, 1.0, 0.0)
        hot = hit.astype(BF16)
        counted = dot(hot, before, NN)
        rank = jnp.sum(hit * (counted[:, :chunk] + running), axis=0, keepdims=True)
        running = running + counted[:, chunk:]
        mine = place == rank
        high = jnp.where(mine, (cell >> 7).astype(F32), 0.0)
        low = jnp.where(mine, (cell & 127).astype(F32), 0.0)
        table = table + dot(hot, jnp.concatenate([high, low], axis=0).astype(BF16), NT)
        share_ref[20:21, span] = owner.astype(F32)
        share_ref[21:22, span] = rank
    asked = (table[:, :CAP] * 128.0 + table[:, CAP:]).astype(jnp.int32)
    request_ref[...] = jnp.concatenate([asked, asked, asked, asked], axis=1)
    for load in loads[2:]:
        load.wait()
    share_ref[0:16, :] = bins_ref[...].astype(F32)
    share_ref[16:19, :] = position_ref[...]
    share_ref[19:20, :] = area_ref[...]
    share_ref[22:24, :] = jnp.zeros((2, panels), F32)


def pack_kernel(at_ref, share_ref, *outs):
    def fold(row):
        line = share_ref[row : row + 1, :]
        return jnp.concatenate([line[:, j * 128 : j * 128 + 128] for j in range(8)], axis=0)

    folded = [fold(row) for row in range(22)]
    for k in range(1, 4):
        to = (at_ref[0] + (4 - k)) % 4
        for b in range(4):
            rows = folded[b]
            for member in range(1, 4):
                rows = jnp.where(to == member, folded[4 * member + b], rows)
            outs[k - 1][b] = rows
        for j in range(6):
            outs[k - 1][4 + j] = folded[16 + j]


def owner_kernel(arrived_ref, fields_ref, reply_ref):
    group = lax.broadcasted_iota(jnp.int32, (32, 128), 1) // CAP
    cells = jnp.zeros((32, 128), jnp.int32)
    for member in range(4):
        cells = jnp.where(group == member, arrived_ref[member * 32 : member * 32 + 32, :], cells)
    block = cells >> 7
    key = ((cells >> 6) & 1) * 128 + ((block >> 5) * 4 + (block & 3)) * 8 + ((block >> 2) & 7)
    spot = cells & 63

    tables = []
    for c in range(4):
        rows = jnp.concatenate(
            [fields_ref[c, x, :, z * 128 : (z + 1) * 128] for x in range(4) for z in range(4)],
            axis=0,
        )
        rows = jnp.transpose(rows)
        rows = jnp.concatenate([rows[:64], rows[64:]], axis=1)
        tables.append(jnp.concatenate(thirds(rows), axis=1).astype(BF16))
    table = jnp.concatenate(tables, axis=0)

    row = lax.broadcasted_iota(jnp.int32, (256, 128), 0).astype(F32).astype(BF16)
    key = key.astype(F32)
    one, none = jnp.ones((), BF16), jnp.zeros((), BF16)
    lane = lax.broadcasted_iota(jnp.int32, (64, 128), 0)
    for g in range(0, 32, 8):
        hot = jnp.concatenate(
            [jnp.where(row == key[g + j : g + j + 1].astype(BF16), one, none) for j in range(8)],
            axis=1,
        )
        looked = dot(table, jnp.concatenate([hot, hot, hot], axis=0), NN)
        for j in range(8):
            mine = lane == spot[g + j : g + j + 1]
            found = jnp.concatenate(
                [
                    jnp.sum(
                        jnp.where(mine, looked[c * 64 : c * 64 + 64, j * 128 : j * 128 + 128], 0.0),
                        axis=0,
                        keepdims=True,
                    )
                    for c in range(4)
                ],
                axis=0,
            )
            for member in range(4):
                turned = found if member == 0 else pltpu.roll(found, 128 - CAP * member, 1)
                reply_ref[member * 32 + g + j] = turned


def thirds(x):
    high = x.astype(BF16).astype(F32)
    rest = x - high
    middle = rest.astype(BF16).astype(F32)
    low = (rest - middle).astype(BF16).astype(F32)
    return high, middle, low


def emit_kernel(scale, returned_ref, *refs):
    *shared_refs, at_ref, observer_ref, signal_ref = refs
    members = len(shared_refs)
    panels = shared_refs[0].shape[1]

    def unfold(ref, row):
        return jnp.concatenate([ref[row, j : j + 1, :] for j in range(8)], axis=1)

    at = at_ref[0]
    observers = observer_ref[:, pl.ds(pl.multiple_of(at * 512, 512), 512)]
    ox, oy, oz = observers[0:1], observers[1:2], observers[2:3]
    none = jnp.zeros_like(ox)
    features = jnp.concatenate(
        [ox, oy, oz, none + 1.0, ox * ox + oy * oy + oz * oz, none, none, none], axis=0
    )
    h, m, w = thirds(features)
    seen = jnp.transpose(jnp.concatenate([h, m, h, m, w, h], axis=0)).astype(BF16)

    table = thirds(
        jnp.concatenate([jnp.transpose(returned_ref[:, c, :]) for c in range(4)], axis=0)
    )[:2]
    device = lax.broadcasted_iota(jnp.int32, (128, panels), 0).astype(F32).astype(BF16)
    place = lax.broadcasted_iota(jnp.int32, (CAP, panels), 0).astype(F32)
    level = lax.broadcasted_iota(jnp.int32, (BINS, panels), 0).astype(F32).astype(BF16)
    zero = jnp.zeros((1, panels), F32)
    one, none = jnp.ones((), BF16), jnp.zeros((), BF16)
    total = [None] * 4
    for member in range(members):
        shared_ref = shared_refs[member]
        if member == 0:
            bins = shared_ref[0:4, :]
            for k in range(1, 4):
                bins = jnp.where(at == k, shared_ref[4 * k : 4 * k + 4, :], bins)
            px, py, pz, area, owner, rank = (shared_ref[16 + j : 17 + j, :] for j in range(6))
        else:
            bins = jnp.concatenate([unfold(shared_ref, b) for b in range(4)], axis=0)
            px, py, pz, area, owner, rank = (unfold(shared_ref, 4 + j) for j in range(6))
        mine = [
            jnp.concatenate(
                [part[c * 128 + member * CAP :][:CAP] for c in range(4)],
                axis=0,
            )
            for part in table
        ]
        rows = jnp.concatenate(mine, axis=1).astype(BF16)
        hot = jnp.where(device == owner.astype(BF16), one, none)
        looked = dot(rows, jnp.concatenate([hot, hot], axis=0), NN)
        here = place == rank
        area = area * scale
        s = [
            area
            * jnp.sum(jnp.where(here, looked[c * CAP : (c + 1) * CAP], 0.0), axis=0, keepdims=True)
            for c in range(4)
        ]
        along = jnp.concatenate(
            [s[1], s[2], s[3], -(s[1] * px + s[2] * py + s[3] * pz), zero, zero, zero, zero], axis=0
        )
        square = jnp.concatenate(
            [-2.0 * px, -2.0 * py, -2.0 * pz, px * px + py * py + pz * pz, zero + 1.0, zero, zero, zero],
            axis=0,
        )
        h, m, w = thirds(along)
        along = jnp.concatenate([h, h, m, m, h, w], axis=0).astype(BF16)
        h, m, w = thirds(square)
        square = jnp.concatenate([h, h, m, m, h, w], axis=0).astype(BF16)
        inverse = lax.rsqrt(dot(seen, square, NN))
        along = dot(seen, along, NN)
        emitted = ((along * inverse + s[0]) * inverse).astype(BF16)
        bins = bins.astype(BF16)
        for b in range(4):
            span = slice(b * OB, (b + 1) * OB)
            hot = jnp.where(bins[b : b + 1] == level, one, none)
            term = dot(emitted[span], hot, NT)
            total[b] = term if member == 0 else total[b] + term
    for b in range(4):
        signal_ref[b * OB : (b + 1) * OB, :] = total[b]


def rim_kernel(odd_ref, fields_ref, velocity_ref, left_ref, right_ref, near_ref, far_ref):
    odd = odd_ref[0] == 1

    def put(spot, low, high):
        near_ref[spot] = jnp.where(odd, low, high)
        far_ref[spot] = jnp.where(odd, high, low)

    for c in range(4):
        for x in range(4):
            column = fields_ref[c, x]
            put(4 * c + x, column[0:4], column[4:8])
        for side in range(2):
            one, two = (
                column_of(fields_ref, left_ref, right_ref, c, x)
                for x in ((-2, -1) if side == 0 else (4, 5))
            )
            put(
                22 + 2 * c + side,
                jnp.concatenate([one[0:2], two[0:2]], axis=0),
                jnp.concatenate([one[6:8], two[6:8]], axis=0),
            )
    for k in range(3):
        for half in range(2):
            one, two = velocity_ref[k, 2 * half], velocity_ref[k, 2 * half + 1]
            put(
                16 + 2 * k + half,
                jnp.concatenate([one[0:2], two[0:2]], axis=0),
                jnp.concatenate([one[6:8], two[6:8]], axis=0),
            )


def column_of(fields_ref, left_ref, right_ref, c, x):
    if x < 0:
        return left_ref[4 * c + x + 4]
    if x >= 4:
        return right_ref[4 * c + x - 4]
    return fields_ref[c, x]


def rate(center, across, tall, velocity, diffusion):
    rows, width = center.shape
    near = [
        (across[2], across[1]),
        (tall[3 : 3 + rows], tall[1 : 1 + rows]),
        (pltpu.roll(center, width - 1, 1), pltpu.roll(center, 1, 1)),
    ]
    far = [
        (across[3], across[0]),
        (tall[4 : 4 + rows], tall[0:rows]),
        (pltpu.roll(center, width - 2, 1), pltpu.roll(center, 2, 1)),
    ]
    advect = 0.0
    spread = -90.0 * center
    for k in range(3):
        advect = advect + velocity[k] * (
            8.0 * (near[k][0] - near[k][1]) - (far[k][0] - far[k][1])
        )
        spread = spread + (16.0 * (near[k][0] + near[k][1]) - (far[k][0] + far[k][1]))
    return (diffusion * spread - advect) * (1.0 / 12.0)


def transport_kernel(
    diffusion_ref, odd_ref, fields_ref, velocity_ref, left_ref, right_ref, near_ref, far_ref, out_ref
):
    odd = odd_ref[0] == 1

    def low(spot):
        return jnp.where(odd, near_ref[spot], far_ref[spot])

    def high(spot):
        return jnp.where(odd, far_ref[spot], near_ref[spot])

    for c in range(4):
        diffusion = diffusion_ref[c]

        def column(x):
            return column_of(fields_ref, left_ref, right_ref, c, x)

        below = {x: low(4 * c + x) for x in range(4)}
        above = {x: high(4 * c + x) for x in range(4)}
        tall = {
            x: jnp.concatenate([below[x][2:4], column(x), above[x][0:2]], axis=0) for x in range(4)
        }
        for side in range(2):
            under, over = low(22 + 2 * c + side), high(22 + 2 * c + side)
            for i in range(2):
                x, part = (-2 + i, 4 + i)[side], slice(2 * i, 2 * i + 2)
                tall[x] = jnp.concatenate([under[part], column(x), over[part]], axis=0)
        middle = {}
        taller = {}
        for x in range(4):
            center = tall[x]
            wide = jnp.concatenate([below[x][0:2], center, above[x][2:4]], axis=0)
            velocity = []
            for k in range(3):
                spot, part = 16 + 2 * k + x // 2, slice(2 * (x % 2), 2 * (x % 2) + 2)
                velocity.append(
                    jnp.concatenate(
                        [low(spot)[part], velocity_ref[k, x], high(spot)[part]], axis=0
                    )
                )
            across = [tall[x + d] for d in (-2, -1, 1, 2)]
            taller[x] = center + TIME_STEP * rate(center, across, wide, velocity, diffusion)
            middle[x] = taller[x][2:10]
        for x in (-2, -1, 4, 5):
            center = column(x)
            side, spot = (left_ref, x + 2) if x < 0 else (right_ref, x - 4)
            velocity = [side[16 + 2 * k + spot] for k in range(3)]
            across = [column(x + d) for d in (-2, -1, 1, 2)]
            middle[x] = center + TIME_STEP * rate(center, across, tall[x], velocity, diffusion)
        for x in range(4):
            velocity = [velocity_ref[k, x] for k in range(3)]
            across = [middle[x + d] for d in (-2, -1, 1, 2)]
            change = rate(middle[x], across, taller[x], velocity, diffusion)
            out_ref[c, x] = 0.5 * fields_ref[c, x] + 0.5 * (middle[x] + TIME_STEP * change)


def neighbours(axis, count, head, tail):
    return (
        lax.ppermute(tail, axis, [(i, (i + 1) % count) for i in range(count)]),
        lax.ppermute(head, axis, [((i + 1) % count, i) for i in range(count)]),
    )


def exchange(array, axes):
    return lax.all_to_all(array, axes, split_axis=0, concat_axis=0, tiled=True)


VM = pl.BlockSpec(memory_space=pltpu.VMEM)
ANY = pl.BlockSpec(memory_space=pl.ANY)
SM = pl.BlockSpec(memory_space=pltpu.SMEM)


def call(kernel, outs, in_specs, args, name, flops, moved, limit=VMEM_LIMIT):
    return pl.pallas_call(
        kernel,
        out_shape=outs,
        in_specs=in_specs,
        out_specs=jax.tree.map(lambda _: VM, outs),
        compiler_params=pltpu.CompilerParams(vmem_limit_bytes=limit),
        cost_estimate=pl.CostEstimate(flops=flops, bytes_accessed=moved, transcendentals=0),
        name=name,
    )(*args)


def ask(owner, cell, bins, position, area, fields, velocity):
    panels = owner.shape[1]
    side = jax.ShapeDtypeStruct((22, 8, 512), F32)
    return pl.pallas_call(
        ask_kernel,
        out_shape=(
            jax.ShapeDtypeStruct((128, 128), jnp.int32),
            jax.ShapeDtypeStruct((24, panels), F32),
            side,
            side,
        ),
        in_specs=[ANY] * 7,
        out_specs=(VM, VM, VM, VM),
        scratch_shapes=[
            pltpu.VMEM((1, panels), jnp.int32),
            pltpu.VMEM((1, panels), jnp.int32),
            pltpu.VMEM((16, panels), jnp.int32),
            pltpu.VMEM((3, panels), F32),
            pltpu.VMEM((1, panels), F32),
            pltpu.SemaphoreType.DMA((19,)),
        ],
        cost_estimate=pl.CostEstimate(flops=2_000_000, bytes_accessed=100_000, transcendentals=0),
        compiler_params=pltpu.CompilerParams(vmem_limit_bytes=FULL_VMEM),
        name="ask",
    )(owner, cell, bins, position, area, fields, velocity)


def per_device(
    fields,
    velocity,
    diffusion,
    panel_owner,
    panel_cell,
    panel_bins,
    panel_position,
    panel_area,
    observer_position,
):
    shape = jax.ShapeDtypeStruct
    after = lax.optimization_barrier
    panels = panel_cell.shape[0]
    every = ("hi", "lo", "gy")
    rims = shape((30, 4, 512), F32)

    requests, share, head, tail = ask(
        panel_owner.reshape(1, panels),
        panel_cell.reshape(1, panels),
        panel_bins,
        panel_position,
        panel_area.reshape(1, panels),
        fields,
        velocity,
    )
    arrived = exchange(requests, every)

    left, right = neighbours(("hi", "lo"), 32, head, tail)
    at = lax.axis_index("hi").reshape(1)
    few = shape((10, 8, 128), F32)
    packed = call(
        pack_kernel,
        (few, few, few),
        [SM, VM],
        (at, share),
        "pack",
        100_000,
        250_000,
    )
    arrived = after((arrived, *packed))[0]
    group = [share]
    for k in range(1, 4):
        group.append(lax.ppermute(packed[k - 1], "hi", [(i, (i - k) % 4) for i in range(4)]))

    reply = call(
        owner_kernel,
        shape((128, 4, 128), F32),
        [VM] * 2,
        (arrived, fields),
        "sample",
        5_000_000_000,
        600_000,
    )
    reply, group[1], group[2] = after((reply, group[1], group[2]))
    returned = exchange(reply, every)

    left, right, _ = after((left, right, reply))
    odd = (lax.axis_index("gy") % 2).reshape(1)
    near, far = call(
        rim_kernel,
        (rims, rims),
        [SM] + [VM] * 4,
        (odd, fields, velocity, left, right),
        "rim",
        100_000,
        2_000_000,
    )
    returned = after((returned, near, far))[0]
    near = lax.ppermute(near, "gy", [(0, 1), (1, 0), (2, 3), (3, 2)])
    far = lax.ppermute(far, "gy", [(1, 2), (2, 1), (3, 0), (0, 3)])

    scale = (BINS / (panels * 128)) ** 0.5
    partial = call(
        functools.partial(emit_kernel, scale),
        shape((512, BINS), F32),
        [VM] * 5 + [SM, VM],
        (returned, *group, at, observer_position),
        "emit",
        5_000_000_000,
        800_000,
    )
    parts = exchange(partial.reshape(32, 16, BINS), ("lo", "gy"))

    near, far, _ = after((near, far, partial))
    advanced = call(
        transport_kernel,
        shape(fields.shape, F32),
        [SM, SM] + [VM] * 6,
        (diffusion, odd, fields, velocity, left, right, near, far),
        "transport",
        5_000_000_000,
        3_000_000,
    )
    parts, advanced = after((parts, advanced))
    return advanced, jnp.sum(parts, axis=0)


def solution(mesh):
    count_x, count_y = mesh.devices.shape
    split = Mesh(mesh.devices.reshape(4, count_x // 4, count_y), ("hi", "lo", "gy"))
    gx = ("hi", "lo")
    every = ("hi", "lo", "gy")

    in_specs = (
        P(None, gx, "gy", None),
        P(None, gx, "gy", None),
        P(),
        P(every, None),
        P(every),
        P(None, every),
        P(None, every),
        P(every),
        P(),
    )
    out_specs = (P(None, gx, "gy", None), P(every, None))
    return jax.shard_map(
        per_device, mesh=split, in_specs=in_specs, out_specs=out_specs, check_vma=False
    )
```
